32 devices in a mesh: fsdp: 4 (over z), seq: 8 (over y, x, core).
Axes of the slice: x: 2, y: 2, z: 4, core: 2. Of those that a mesh axis runs over, the one named last changes fastest.
Arguments:
- hidden_in: bfloat16 [2, 2048, 2048], P(None, 'seq', 'fsdp'), may hold values from -6 to 6
- out_cot: bfloat16 [2, 2048, 2048], P(None, 'seq', 'fsdp'), may hold values from -6 to 6
- doc_lengths: int32 [2, 16], replicated, may hold values from 1 to 1024, 2048 in all within a row
- mixer_gain: float32 [2048], replicated, may hold values from 0.5 to 1.5
- in_proj: bfloat16 [2048, 3, 2048], P('seq', None, 'fsdp'), may hold values from -0.125 to 0.125
- short_filter: float32 [3, 3, 2048], P(None, None, 'fsdp'), may hold values from -3 to 3
- decay_rate: float32 [2048, 16], P('fsdp'), may hold values from 9.765625e-06 to 0.05
- mode_angle: float32 [2048, 16], P('fsdp'), may hold values from -0.05 to 0.05
- residue_re: float32 [2048, 16], P('fsdp'), may hold values from -0.25 to 0.25
- residue_im: float32 [2048, 16], P('fsdp'), may hold values from -0.25 to 0.25
- skip_gain: float32 [2048], P('fsdp'), may hold values from 0.5 to 1.5
- out_proj: bfloat16 [2048, 2048], P('fsdp', 'seq'), may hold values from -0.125 to 0.125
- feed_gain: float32 [2048], replicated, may hold values from 0.5 to 1.5
- gate_proj: bfloat16 [2048, 5632], P('seq', 'fsdp'), may hold values from -0.125 to 0.125
- up_proj: bfloat16 [2048, 5632], P('seq', 'fsdp'), may hold values from -0.125 to 0.125
- down_proj: bfloat16 [5632, 2048], P('fsdp', 'seq'), may hold values from -0.109375 to 0.109375
Outputs:
- block_out: bfloat16 [2, 2048, 2048], P(None, 'seq', 'fsdp')
- hidden_grad: float32 [2, 2048, 2048], P(None, 'seq', 'fsdp')
- mixer_gain_grad: float32 [2048], replicated
- in_proj_grad: float32 [2048, 3, 2048], P('seq', None, 'fsdp')
- short_filter_grad: float32 [3, 3, 2048], P(None, None, 'fsdp')
- decay_rate_grad: float32 [2048, 16], P('fsdp')
- mode_angle_grad: float32 [2048, 16], P('fsdp')
- residue_re_grad: float32 [2048, 16], P('fsdp')
- residue_im_grad: float32 [2048, 16], P('fsdp')
- skip_gain_grad: float32 [2048], P('fsdp')
- out_proj_grad: float32 [2048, 2048], P('fsdp', 'seq')
- feed_gain_grad: float32 [2048], replicated
- gate_proj_grad: float32 [2048, 5632], P('seq', 'fsdp')
- up_proj_grad: float32 [2048, 5632], P('seq', 'fsdp')
- down_proj_grad: float32 [5632, 2048], P('fsdp', 'seq')
The draws below stay inside these ranges and needn't reach their ends.
Inputs may be any that keep to these rules, and one draw needn't show every extreme that they name: `doc_lengths`: each row lists the 16 documents of one micro-batch in order; they sum to 2048 tokens and one of them is exactly 1024 long.
All inputs are finite; a program needn't handle non-finite values.
Results may differ from the reference program's by a relative error of at most 0.017.
Values may be sent and summed in bfloat16 or wider, within the bound.
No kernel may reach another device: no remote copies, remote signals or barrier semaphores. Data moves between devices by JAX's collectives and lax.ppermute only.
A program may use at most 320 MiB of HBM per device.

```python
import math
import jax
import jax.numpy as jnp
import numpy as np
from jax import lax

D = 2048
FF = 5632
MODES = 16
MB = 2
NDOCS = 16
LEN = 2048
DOC_MAX = 1024


def block_levels(rng, dims, cuts, low, high):
    gain, own = 1.0, jax.random.fold_in(rng, 6)
    for dim, blocks in cuts:
        steps = jnp.exp(jax.random.uniform(jax.random.fold_in(own, dim), (blocks,), jnp.float32, low / len(cuts), high / len(cuts)))
        gain = gain * jnp.repeat(steps, dims[dim] // blocks).reshape([-1 if axis == dim else 1 for axis in range(len(dims))])
    return gain


def profile(count, total, limit, slope):
    weights = [(1 << 20) // math.isqrt(rank ** slope) + 1 for rank in range(2, count + 1)]
    rest, counts = total - limit - (count - 1), [1] * (count - 1)
    while rest > 0:
        movable = [i for i in range(count - 1) if counts[i] < limit]
        whole, remaining = sum([weights[i] for i in movable]), rest
        for i in movable:
            more = min(limit - counts[i], max(1, remaining * weights[i] // whole), rest)
            counts[i] = counts[i] + more
            rest = rest - more
    return np.array([limit] + counts)


def uneven(own_key, count, total, most, lean):
    if count == 2:
        one = jax.random.randint(own_key, (), max(1, total - most), min(most, total - 1) + 1)
        return jnp.stack([one, total - one])
    tallies = jnp.asarray(profile(count, total, most, lean), jnp.int32)
    twos = (count - 1) // 2
    donor, receiver = tallies[1:1 + 2 * twos:2], tallies[2:2 + 2 * twos:2]
    margin = jnp.minimum(donor - 1, most - receiver)
    moved = jax.random.randint(jax.random.fold_in(own_key, 1), (twos,), 0, 1 << 20) % (margin + 1)
    tallies = tallies.at[1:1 + 2 * twos:2].set(donor - moved).at[2:2 + 2 * twos:2].set(receiver + moved)
    return tallies[jax.random.permutation(jax.random.fold_in(own_key, 2), count)]


def bell_draw(key, shape, scale, most, shards=(), kind=jnp.bfloat16):
    level = block_levels(key, shape, shards, -0.22, 0.18) if shards else 1.0
    values = jax.random.normal(key, shape, jnp.float32) * scale * level
    return jnp.minimum(jnp.maximum(values, -most), most).astype(kind)


def setup_inputs(seed: int = 0) -> dict:
    key_of = jax.random.split(jax.random.key(seed), 17)
    return {
        "hidden_in": bell_draw(key_of[0], (MB, LEN, D), 1.0, 6.0, ((1, 8), (2, 4))),
        "out_cot": bell_draw(key_of[1], (MB, LEN, D), 1.0, 6.0, ((1, 8), (2, 4))),
        "doc_lengths": jax.vmap(lambda own: uneven(own, NDOCS, LEN, DOC_MAX, 2))(jax.random.split(key_of[2], MB)).reshape((MB, NDOCS)).astype(jnp.int32),
        "mixer_gain": jnp.clip(1.0 + 0.1 * jax.random.normal(key_of[3], (D,), jnp.float32), 0.5, 1.5),
        "in_proj": bell_draw(key_of[4], (D, 3, D), D ** -0.5, 0.125, ((0, 8), (2, 4))),
        "short_filter": bell_draw(key_of[5], (3, 3, D), 0.6, 3.0, ((2, 4),), jnp.float32),
        "decay_rate": jnp.clip(jnp.exp(math.log(0.05) - 8.54091 * jax.random.uniform(key_of[6], (D, MODES), jnp.float32) ** block_levels(key_of[6], (D, MODES), ((0, 4),), -0.2, 0.2)), 9.765624781721272e-06, 0.05),
        "mode_angle": jnp.clip(jax.random.uniform(key_of[7], (D, MODES), jnp.float32, -0.05, 0.05) * block_levels(key_of[7], (D, MODES), ((0, 4),), -0.4, 0.0), -0.05, 0.05),
        "residue_re": bell_draw(key_of[8], (D, MODES), (2.0 / (MODES * DOC_MAX) ** 0.5), 0.25, ((0, 4),), jnp.float32),
        "residue_im": bell_draw(key_of[9], (D, MODES), (2.0 / (MODES * DOC_MAX) ** 0.5), 0.25, ((0, 4),), jnp.float32),
        "skip_gain": jnp.clip(0.5 + 1.0 * jax.random.uniform(key_of[10], (D,), jnp.float32) ** block_levels(key_of[10], (D,), ((0, 4),), -0.2, 0.2), 0.5, 1.5),
        "out_proj": bell_draw(key_of[11], (D, D), D ** -0.5, 0.125, ((0, 4), (1, 8))),
        "feed_gain": jnp.clip(1.0 + 0.1 * jax.random.normal(key_of[12], (D,), jnp.float32), 0.5, 1.5),
        "gate_proj": bell_draw(key_of[13], (D, FF), D ** -0.5, 0.125, ((0, 8), (1, 4))),
        "up_proj": bell_draw(key_of[14], (D, FF), D ** -0.5, 0.125, ((0, 8), (1, 4))),
        "down_proj": bell_draw(key_of[15], (FF, D), (FF // 2) ** -0.5, 0.109375, ((0, 4), (1, 8))),
    }


norm_eps = 1e-05
block_len = 64
highest = lax.Precision.HIGHEST

@jax.custom_vjp
def low(v):
    return lax.optimization_barrier(v.astype(jnp.bfloat16)).astype(jnp.float32)

@jax.custom_vjp
def low_back(v):
    return v

def low_keep(v):
    return (low(v), None)

def low_pass(kept, grad):
    return (grad,)

def back_keep(v):
    return (v, None)

def back_low(kept, grad):
    return (low(grad),)
low.defvjp(low_keep, low_pass)
low_back.defvjp(back_keep, back_low)

def doc_tables(doc_lens, total):
    places = jnp.arange(total, dtype=jnp.int32)
    starts = (jnp.cumsum(doc_lens, dtype=jnp.int32) - doc_lens).astype(jnp.int32)
    before = starts[None, :] <= places[:, None]
    doc_ids = (lax.optimization_barrier(jnp.sum(before.astype(jnp.int32), axis=1, dtype=jnp.int32)) - 1).astype(jnp.int32)
    begins = lax.optimization_barrier(jnp.max(jnp.where(before, starts[None, :], 0), axis=1)).astype(jnp.int32)
    return (doc_ids, (places - begins).astype(jnp.int32))

def chain_step(earlier_part, later_part):
    early_mul_re, early_mul_im, early_sum_re, early_sum_im = earlier_part
    late_mul_re, late_mul_im, late_sum_re, late_sum_im = later_part
    return (late_mul_re * early_mul_re - late_mul_im * early_mul_im, late_mul_re * early_mul_im + late_mul_im * early_mul_re, late_mul_re * early_sum_re - late_mul_im * early_sum_im + late_sum_re, late_mul_re * early_sum_im + late_mul_im * early_sum_re + late_sum_im)

def conv_group(values, doc_ids, rates, angles, res_real, res_imag):
    length, group = values.shape
    count = length // block_len
    ramp = jnp.arange(block_len + 1, dtype=jnp.float32)
    fading = jnp.exp(-rates[:, :, None] * ramp)
    pow_re = fading * jnp.cos(angles[:, :, None] * ramp)
    pow_im = fading * jnp.sin(angles[:, :, None] * ramp)
    within = jnp.arange(block_len, dtype=jnp.int32)
    spread = within[:, None] - within[None, :]
    lags = jnp.maximum(spread, 0).astype(jnp.float32)
    kernel = jnp.exp(-rates[:, :, None, None] * lags) * (res_real[:, :, None, None] * jnp.cos(angles[:, :, None, None] * lags) - res_imag[:, :, None, None] * jnp.sin(angles[:, :, None, None] * lags))
    toeplitz = lax.optimization_barrier(jnp.sum(kernel, axis=1))
    blocks = values.reshape(count, block_len, group)
    doc_blocks = doc_ids.reshape(count, block_len)
    same_doc = ((doc_blocks[:, :, None] == doc_blocks[:, None, :]) & (spread >= 0)[None]).astype(jnp.float32)
    masked = toeplitz[None] * same_doc[:, None]
    inner = jnp.einsum('bgts,bsg->btg', masked, blocks, precision=highest)
    ends = doc_blocks[:, -1]
    earlier = jnp.concatenate([jnp.full((1,), -1, dtype=jnp.int32), ends[:-1].astype(jnp.int32)])
    tail = (doc_blocks == ends[:, None]).astype(jnp.float32)
    rev_re = pow_re[:, :, block_len - 1::-1]
    rev_im = pow_im[:, :, block_len - 1::-1]
    weighted = blocks * tail[:, :, None]
    end_re = jnp.einsum('bjg,gkj->bgk', weighted, rev_re, precision=highest)
    end_im = jnp.einsum('bjg,gkj->bgk', weighted, rev_im, precision=highest)
    keep = (ends == earlier).astype(jnp.float32)[:, None, None]
    carry_re = keep * pow_re[None, :, :, block_len]
    carry_im = keep * pow_im[None, :, :, block_len]
    scanned = lax.associative_scan(chain_step, (carry_re, carry_im, end_re, end_im), axis=0)
    state_re, state_im = (scanned[2], scanned[3])
    zero_state = jnp.zeros((1,) + state_re.shape[1:], dtype=jnp.float32)
    prior_re = jnp.concatenate([zero_state, state_re[:-1]], axis=0)
    prior_im = jnp.concatenate([zero_state, state_im[:-1]], axis=0)
    coef_re = res_real[None] * prior_re - res_imag[None] * prior_im
    coef_im = res_real[None] * prior_im + res_imag[None] * prior_re
    outer = jnp.einsum('bgk,gkj->bjg', coef_re, pow_re[:, :, 1:], precision=highest) - jnp.einsum('bgk,gkj->bjg', coef_im, pow_im[:, :, 1:], precision=highest)
    alive = (doc_blocks == earlier[:, None]).astype(jnp.float32)
    return (inner + outer * alive[:, :, None]).reshape(length, group)

def long_conv(values, doc_ids, rates, angles, res_real, res_imag, skip_part):
    length, chans = values.shape
    group = math.gcd(chans, 16)
    folds = chans // group
    stacked = values.reshape(length, folds, group).transpose(1, 0, 2)

    def per_group(items):
        return conv_group(items[0], doc_ids, items[1], items[2], items[3], items[4])
    mapped = lax.map(jax.checkpoint(per_group), (stacked, rates.reshape(folds, group, -1), angles.reshape(folds, group, -1), res_real.reshape(folds, group, -1), res_imag.reshape(folds, group, -1)))
    return mapped.transpose(1, 0, 2).reshape(length, chans) + skip_part[None, :] * values

def rms_scale(values):
    return lax.rsqrt(lax.optimization_barrier(jnp.mean(values * values, axis=-1, keepdims=True)) + norm_eps)

def one_batch(resid, doc_ids, places, mixer_gain, in_proj, short_filter, decay_rate, mode_angle, residue_re, residue_im, skip_gain, out_proj, feed_gain, gate_proj, up_proj, down_proj):
    length = resid.shape[0]
    normed_one = low(resid * rms_scale(resid) * mixer_gain)
    project = low_back(jnp.einsum('td,dje->tje', normed_one, in_proj, precision=highest))
    conv_out = jnp.zeros_like(project)
    for lag_tap in range(3):
        shifted = jnp.pad(project, ((lag_tap, 0), (0, 0), (0, 0)))[:length]
        valid = (places >= lag_tap).astype(jnp.float32)
        conv_out = conv_out + short_filter[lag_tap][None] * shifted * valid[:, None, None]
    product = low(low_back(conv_out[:, 1] * conv_out[:, 2]))
    mixed = low(low_back(long_conv(product, doc_ids, decay_rate, mode_angle, residue_re, residue_im, skip_gain)))
    gated = low(conv_out[:, 0] * mixed)
    mix_out = low_back(jnp.dot(gated, out_proj, precision=highest))
    stream = resid + mix_out
    normed_two = low(stream * rms_scale(stream) * feed_gain)
    gate_pre = low_back(jnp.dot(normed_two, gate_proj, precision=highest))
    up_pre = low_back(jnp.dot(normed_two, up_proj, precision=highest))
    hidden = low(jax.nn.silu(gate_pre) * up_pre)
    return stream + jnp.dot(hidden, down_proj, precision=highest)

def reference(hidden_in, out_cot, doc_lengths, mixer_gain, in_proj, short_filter, decay_rate, mode_angle, residue_re, residue_im, skip_gain, out_proj, feed_gain, gate_proj, up_proj, down_proj):
    batches = hidden_in.shape[0]
    tables = [doc_tables(doc_lengths[micro], hidden_in.shape[1]) for micro in range(batches)]

    def forward(hidden, gain_one, w_in, taps, rates, angles, res_real, res_imag, skips, w_out, gain_two, w_gate, w_up, w_down):
        pieces = [jax.checkpoint(one_batch)(hidden[micro], tables[micro][0], tables[micro][1], gain_one, w_in, taps, rates, angles, res_real, res_imag, skips, w_out, gain_two, w_gate, w_up, w_down) for micro in range(batches)]
        return jnp.stack(pieces)
    result, backward = jax.vjp(forward, hidden_in.astype(jnp.float32), mixer_gain, in_proj.astype(jnp.float32), short_filter, decay_rate, mode_angle, residue_re, residue_im, skip_gain, out_proj.astype(jnp.float32), feed_gain, gate_proj.astype(jnp.float32), up_proj.astype(jnp.float32), down_proj.astype(jnp.float32))
    grads = backward(out_cot.astype(jnp.float32))
    return (result.astype(jnp.bfloat16), grads[0], grads[1], grads[2], grads[3], grads[4], grads[5], grads[6], grads[7], grads[8], grads[9], grads[10], grads[11], grads[12], grads[13])
```

```python
import functools

import jax
import jax.numpy as jnp
from jax import lax
from jax.experimental import pallas as pl
from jax.experimental.pallas import tpu as pltpu
from jax.sharding import PartitionSpec as P

norm_eps = 1e-05
half_modes = 8
f32 = jnp.float32
bf16 = jnp.bfloat16


def widen(src_ref, dst_ref, count):
    total, chans = src_ref.shape[0], src_ref.shape[1] // count
    rows = min(256, total)

    def body(block, _):
        base = pl.multiple_of(block * rows, rows)
        part = src_ref[pl.ds(base, rows), :].astype(f32)
        for m in range(count):
            own = part[:, m * chans : (m + 1) * chans]
            dst_ref[m, pl.ds(base, rows), :] = jnp.concatenate([own, own], axis=1)
        return 0

    lax.fori_loop(0, total // rows, body, 0)


def narrow(src_ref, direct_ref, skip, dst_ref, count):
    total, chans = direct_ref.shape[0], direct_ref.shape[1] // count
    rows = min(256, total)

    def body(block, _):
        base = pl.multiple_of(block * rows, rows)
        parts = []
        for m in range(count):
            wide = src_ref[m, pl.ds(base, rows), :]
            parts.append(wide[:, :chans] + wide[:, chans:])
        summed = jnp.concatenate(parts, axis=1) if count > 1 else parts[0]
        direct = direct_ref[pl.ds(base, rows), :].astype(f32)
        dst_ref[pl.ds(base, rows), :] = (summed + skip * direct).astype(bf16)
        return 0

    lax.fori_loop(0, total // rows, body, 0)


def scan_kernel(count, step, keep_ref, u_ref, par_ref, skip_ref, y_ref, u_wide, y_wide):
    total = u_ref.shape[0]
    turn_re, turn_im, res_re, res_im = (par_ref[i] for i in range(4))
    widen(u_ref, u_wide, count)

    def body(block, states):
        states = list(states)
        base = pl.multiple_of(block * step, step)
        for i in range(step):
            for m in range(count):
                x_re, x_im = states[m]
                keep = keep_ref[m, base + i]
                mul_re, mul_im = turn_re * keep, turn_im * keep
                new_re = mul_re * x_re + (u_wide[m, pl.ds(base + i, 1), :] - mul_im * x_im)
                new_im = mul_re * x_im + mul_im * x_re
                y_wide[m, pl.ds(base + i, 1), :] = jnp.sum(
                    res_re * new_re - res_im * new_im, axis=0, keepdims=True
                )
                states[m] = (new_re, new_im)
        return tuple(states)

    zero = jnp.zeros(turn_re.shape, f32)
    lax.fori_loop(0, total // step, body, tuple((zero, zero) for _ in range(count)))
    narrow(y_wide, u_ref, skip_ref[...], y_ref, count)


def back_kernel(
    count, step, keep_ref, u_ref, g_ref, par_ref, skip_ref, d_ref, sums_ref, skip_sum_ref, u_wide, g_wide, d_wide
):
    total = u_ref.shape[0]
    blocks = total // step
    turn_re, turn_im, res_re, res_im = (par_ref[i] for i in range(4))
    zero = jnp.zeros(turn_re.shape, f32)
    widen(u_ref, u_wide, count)
    widen(g_ref, g_wide, count)

    def body(block, carry):
        ahead, behind, sums = list(carry[0]), list(carry[1]), carry[2]
        base = pl.multiple_of(block * step, step)
        rear = pl.multiple_of((blocks - 1 - block) * step, step)
        for i in range(step):
            j = step - 1 - i
            for m in range(count):
                x_re, x_im, w_re, w_im = ahead[m]
                keep = keep_ref[m, base + i]
                mul_re, mul_im = turn_re * keep, turn_im * keep
                sum_re, sum_im = w_re + x_re, w_im + x_im
                w_re, w_im = mul_re * sum_re - mul_im * sum_im, mul_re * sum_im + mul_im * sum_re
                x_re, x_im = (
                    mul_re * x_re + (u_wide[m, pl.ds(base + i, 1), :] - mul_im * x_im),
                    mul_re * x_im + mul_im * x_re,
                )
                ahead[m] = (x_re, x_im, w_re, w_im)
                cot = g_wide[m, pl.ds(base + i, 1), :]
                sums = (
                    sums[0] + cot * x_re,
                    sums[1] + cot * x_im,
                    sums[2] + cot * w_re,
                    sums[3] + cot * w_im,
                )
                z_re, z_im, keep = behind[m]
                mul_re, mul_im = turn_re * keep, turn_im * keep
                z_re, z_im = (
                    mul_re * z_re + (g_wide[m, pl.ds(rear + j, 1), :] - mul_im * z_im),
                    mul_re * z_im + mul_im * z_re,
                )
                behind[m] = (z_re, z_im, keep_ref[m, rear + j])
                d_wide[m, pl.ds(rear + j, 1), :] = jnp.sum(res_re * z_re - res_im * z_im, axis=0, keepdims=True)
        return tuple(ahead), tuple(behind), sums

    start = (
        tuple((zero, zero, zero, zero) for _ in range(count)),
        tuple((zero, zero, jnp.float32(0)) for _ in range(count)),
        (zero, zero, zero, zero),
    )
    _, _, (g_re, g_im, lag_re, lag_im) = lax.fori_loop(0, blocks, body, start)
    sums_ref[0] = res_im * lag_im - res_re * lag_re
    sums_ref[1] = zero - (res_re * lag_im + res_im * lag_re)
    sums_ref[2] = g_re
    sums_ref[3] = zero - g_im
    narrow(d_wide, g_ref, skip_ref[...], d_ref, count)
    skip_sum_ref[...] = jnp.sum(u_ref[...].astype(f32) * g_ref[...].astype(f32), axis=0, keepdims=True)


def in_vmem():
    return pl.BlockSpec(memory_space=pltpu.VMEM)


def long_conv(u, keep, params, skips, count):
    total, width = u.shape
    return pl.pallas_call(
        functools.partial(scan_kernel, count, 16),
        out_shape=jax.ShapeDtypeStruct(u.shape, bf16),
        in_specs=[pl.BlockSpec(memory_space=pltpu.SMEM)] + [in_vmem()] * 3,
        out_specs=in_vmem(),
        scratch_shapes=[pltpu.VMEM((count, total, 2 * width // count), f32)] * 2,
        compiler_params=pltpu.CompilerParams(vmem_limit_bytes=48 << 20),
    )(keep, u, params, skips)


def long_conv_back(u, g, keep, params, skips, count):
    total, width = u.shape
    return pl.pallas_call(
        functools.partial(back_kernel, count, 16),
        out_shape=(
            jax.ShapeDtypeStruct(u.shape, bf16),
            jax.ShapeDtypeStruct(params.shape, f32),
            jax.ShapeDtypeStruct((1, width), f32),
        ),
        in_specs=[pl.BlockSpec(memory_space=pltpu.SMEM)] + [in_vmem()] * 4,
        out_specs=(in_vmem(),) * 3,
        scratch_shapes=[pltpu.VMEM((count, total, 2 * width // count), f32)] * 3,
        compiler_params=pltpu.CompilerParams(vmem_limit_bytes=48 << 20),
    )(keep, u, g, params, skips)


def pack_modes(rates, angles, res_re, res_im):
    def on_lanes(part):
        turned = part.T
        return jnp.concatenate([turned[:half_modes], turned[half_modes:]], axis=1)

    fading = jnp.exp(-rates)
    return jnp.stack(
        [on_lanes(part) for part in (fading * jnp.cos(angles), fading * jnp.sin(angles), res_re, res_im)]
    )


def shifted(array, axis, by):
    size = lax.axis_size(axis)
    pairs = [(i, i + by) for i in range(size) if 0 <= i + by < size]
    return lax.ppermute(array, axis, pairs)


def places_of(doc_lens, total):
    tokens = jnp.arange(total, dtype=jnp.int32)
    starts = jnp.cumsum(doc_lens, dtype=jnp.int32) - doc_lens
    begins = jnp.max(jnp.where(starts[None, :] <= tokens[:, None], starts[None, :], 0), axis=1)
    return tokens - begins


def dot_rows(left, right):
    return lax.dot_general(left, right, (((1,), (1,)), ((), ())), preferred_element_type=f32)


def dot_tokens(left, right):
    return lax.dot_general(left, right, (((0,), (0,)), ((), ())), preferred_element_type=f32)


def dot(left, right):
    return jnp.dot(left, right, preferred_element_type=f32)


def gather_share(share):
    return lax.all_gather(share, "fsdp", axis=1, tiled=True)


def scatter_share(partial_sums):
    return lax.psum_scatter(partial_sums.astype(bf16), "fsdp", scatter_dimension=1, tiled=True).astype(f32)


def gather_weight(shard):
    return lax.all_gather(shard, "seq", axis=0, tiled=True)


def scatter_weight(grad):
    return lax.psum_scatter(grad.astype(bf16), "seq", scatter_dimension=0, tiled=True).astype(f32)


def to_channels(token_side, batches):
    rows, chans = token_side.shape[0] // batches, token_side.shape[1]
    count = lax.axis_size("seq")
    part = chans // count
    pieces = token_side.reshape(batches, rows, count, part).transpose(2, 1, 0, 3)
    sent = lax.all_to_all(pieces.reshape(count, rows, batches * part), "seq", split_axis=0, concat_axis=0)
    return sent.reshape(count * rows, batches * part)


def to_tokens(channel_side, batches):
    total, width = channel_side.shape
    count = lax.axis_size("seq")
    rows, part = total // count, width // batches
    sent = lax.all_to_all(channel_side.reshape(count, rows, width), "seq", split_axis=0, concat_axis=0)
    return sent.reshape(count, rows, batches, part).transpose(2, 1, 0, 3).reshape(batches * rows, count * part)


def on_device(
    hidden_in,
    out_cot,
    doc_lengths,
    mixer_gain,
    in_proj,
    short_filter,
    decay_rate,
    mode_angle,
    residue_re,
    residue_im,
    skip_gain,
    out_proj,
    feed_gain,
    gate_proj,
    up_proj,
    down_proj,
):
    batches, rows, share = hidden_in.shape
    tokens = batches * rows
    width = mixer_gain.shape[0]
    seq_count = lax.axis_size("seq")
    seq_rank = lax.axis_index("seq")
    fsdp_rank = lax.axis_index("fsdp")
    total = rows * seq_count
    chan_here = share // seq_count
    d_rows = in_proj.shape[0]

    x_share = hidden_in.reshape(tokens, share)
    cot_share = out_cot.reshape(tokens, share)
    x_all = gather_share(x_share).astype(f32)
    w_in = gather_weight(in_proj.reshape(d_rows, 3 * share))
    w_out = gather_weight(out_proj.T)
    w_gate = gather_weight(gate_proj)
    w_up = gather_weight(up_proj)
    w_down = gather_weight(down_proj.T)
    cot_all = gather_share(cot_share)

    places = jnp.stack([places_of(doc_lengths[m], total) for m in range(batches)])
    keep = (places > 0).astype(f32)
    places_here = lax.dynamic_slice_in_dim(places, seq_rank * rows, rows, 1)
    masks = [(places_here >= lag).astype(f32)[:, :, None] for lag in range(3)]
    taps = short_filter.reshape(3, 3 * share)

    def own_channels(part):
        return lax.dynamic_slice_in_dim(part, seq_rank * chan_here, chan_here, 0)

    modes = pack_modes(*(own_channels(part) for part in (decay_rate, mode_angle, residue_re, residue_im)))
    skips = jnp.tile(own_channels(skip_gain), batches)[None]

    scale_one = lax.rsqrt(jnp.mean(x_all * x_all, axis=-1, keepdims=True) + norm_eps)
    unit_one = x_all * scale_one
    normed_one = (unit_one * mixer_gain).astype(bf16)
    project = dot(normed_one, w_in).reshape(batches, rows, 3 * share)
    extended = jnp.concatenate([shifted(project[:, -2:], "seq", 1), project], axis=1)
    lagged = [extended[:, 2 - lag : 2 - lag + rows] for lag in range(3)]
    conv = sum(taps[lag] * masks[lag] * lagged[lag] for lag in range(3)).reshape(tokens, 3 * share)
    gate_one, gate_two, values = (conv[:, j * share : (j + 1) * share] for j in range(3))
    channel_in = to_channels((gate_two * values).astype(bf16), batches)
    channel_out = long_conv(channel_in, keep, modes, skips, batches)
    mixed = to_tokens(channel_out, batches).astype(f32)
    gated = (gate_one * mixed).astype(bf16)
    stream = x_share.astype(f32) + scatter_share(dot_rows(gated, w_out))
    stream_all = gather_share(stream.astype(bf16)).astype(f32)
    scale_two = lax.rsqrt(jnp.mean(stream_all * stream_all, axis=-1, keepdims=True) + norm_eps)
    unit_two = stream_all * scale_two
    normed_two = (unit_two * feed_gain).astype(bf16)
    gate_pre = dot(normed_two, w_gate)
    up_pre = dot(normed_two, w_up)
    sigmoid = jax.nn.sigmoid(gate_pre)
    activated = gate_pre * sigmoid
    hidden = (activated * up_pre).astype(bf16)
    block_out = stream + scatter_share(dot_rows(hidden, w_down))

    d_hidden = dot(cot_all, w_down)
    d_gate = (d_hidden * up_pre * sigmoid * (1.0 + gate_pre * (1.0 - sigmoid))).astype(bf16)
    d_up = (d_hidden * activated).astype(bf16)
    grad_down = dot_tokens(cot_all, hidden)
    grad_gate = dot_tokens(normed_two, d_gate)
    grad_up = dot_tokens(normed_two, d_up)
    part_two = dot_rows(d_gate, w_gate) + dot_rows(d_up, w_up)
    along_two = lax.psum(
        jnp.sum(d_gate.astype(f32) * gate_pre + d_up.astype(f32) * up_pre, axis=-1, keepdims=True), "fsdp"
    )
    feed_gain_part = jnp.sum(unit_two * part_two, axis=0)

    def own_features(part):
        return lax.dynamic_slice_in_dim(part, fsdp_rank * share, share, 0)

    d_stream = (
        cot_share.astype(f32)
        + scale_two * own_features(feed_gain) * scatter_share(part_two)
        - stream * (scale_two * scale_two * along_two / width)
    )
    d_mix = gather_share(d_stream.astype(bf16))

    grad_out = dot_tokens(d_mix, gated)
    d_gated = dot(d_mix, w_out)
    d_gate_one = d_gated * mixed
    back_in = to_channels((d_gated * gate_one).astype(bf16), batches)
    back_out, mode_sums, skip_sums = long_conv_back(channel_in, back_in, keep, modes, skips, batches)
    d_product = to_tokens(back_out, batches).astype(f32)
    d_conv = jnp.concatenate([d_gate_one, d_product * values, d_product * gate_two], axis=1)
    d_conv = d_conv.reshape(batches, rows, 3 * share)
    short_part = jnp.stack([jnp.sum(masks[lag] * lagged[lag] * d_conv, axis=(0, 1)) for lag in range(3)])
    spread = sum(
        jnp.pad(taps[lag] * masks[lag] * d_conv, ((0, 0), (2 - lag, lag), (0, 0))) for lag in range(3)
    )
    returned = shifted(spread[:, :2], "seq", -1)
    d_project = spread[:, 2:] + jnp.pad(returned, ((0, 0), (rows - 2, 0), (0, 0)))
    d_project = d_project.astype(bf16).reshape(tokens, 3 * share)
    along_one = lax.psum(
        jnp.sum(d_project.astype(f32) * project.reshape(tokens, 3 * share), axis=-1, keepdims=True), "fsdp"
    )
    grad_in = dot_tokens(normed_one, d_project)
    part_one = dot_rows(d_project, w_in)
    mixer_gain_part = jnp.sum(unit_one * part_one, axis=0)
    d_x = (
        d_stream
        + scale_one * own_features(mixer_gain) * scatter_share(part_one)
        - x_share.astype(f32) * (scale_one * scale_one * along_one / width)
    )

    in_grad = scatter_weight(grad_in).reshape(d_rows, 3, share)
    out_grad = scatter_weight(grad_out).T
    gate_grad = scatter_weight(grad_gate)
    up_grad = scatter_weight(grad_up)
    down_grad = scatter_weight(grad_down).T
    gains = lax.psum(jnp.stack([mixer_gain_part, feed_gain_part]), ("fsdp", "seq"))
    short_grad = lax.psum(short_part, "seq").reshape(3, 3, share)
    skip_own = jnp.sum(skip_sums.reshape(batches, chan_here), axis=0)
    skip_rows = jnp.zeros((half_modes, 2 * chan_here), f32).at[0, :chan_here].set(skip_own)
    filters = jnp.concatenate([mode_sums, skip_rows[None]], axis=0)
    filters = lax.all_gather(filters, "seq", axis=0)
    by_chan = filters.reshape(seq_count, 5, half_modes, 2, chan_here).transpose(1, 0, 4, 3, 2)
    by_chan = by_chan.reshape(5, share, 2 * half_modes)
    return (
        block_out.astype(bf16).reshape(hidden_in.shape),
        d_x.reshape(hidden_in.shape),
        gains[0],
        in_grad,
        short_grad,
        by_chan[0],
        by_chan[1],
        by_chan[2],
        by_chan[3],
        by_chan[4, :, 0],
        out_grad,
        gains[1],
        gate_grad,
        up_grad,
        down_grad,
    )


def solution(mesh):
    tokens = P(None, "seq", "fsdp")
    chan_rows = P("fsdp", None)
    d_rows = P("seq", "fsdp")
    d_cols = P("fsdp", "seq")
    in_specs = (
        tokens,
        tokens,
        P(),
        P(),
        P("seq", None, "fsdp"),
        P(None, None, "fsdp"),
        chan_rows,
        chan_rows,
        chan_rows,
        chan_rows,
        P("fsdp"),
        d_cols,
        P(),
        d_rows,
        d_rows,
        d_cols,
    )
    out_specs = (
        tokens,
        tokens,
        P(),
        P("seq", None, "fsdp"),
        P(None, None, "fsdp"),
        chan_rows,
        chan_rows,
        chan_rows,
        chan_rows,
        P("fsdp"),
        d_cols,
        P(),
        d_rows,
        d_rows,
        d_cols,
    )
    return jax.shard_map(on_device, mesh=mesh, in_specs=in_specs, out_specs=out_specs, check_vma=False)
```

```python
import functools

import jax
import jax.numpy as jnp
from jax import lax
from jax.experimental import pallas as pl
from jax.experimental.pallas import tpu as pltpu
from jax.sharding import PartitionSpec as P

norm_eps = 1e-05
half_modes = 8
f32 = jnp.float32
bf16 = jnp.bfloat16


def widen(src_ref, dst_ref, count):
    total, chans = src_ref.shape[0], src_ref.shape[1] // count
    rows = min(256, total)

    def body(block, _):
        base = pl.multiple_of(block * rows, rows)
        part = src_ref[pl.ds(base, rows), :].astype(f32)
        for m in range(count):
            own = part[:, m * chans : (m + 1) * chans]
            dst_ref[m, pl.ds(base, rows), :] = jnp.concatenate([own, own], axis=1)
        return 0

    lax.fori_loop(0, total // rows, body, 0)


def narrow(src_ref, direct_ref, skip, dst_ref, count):
    total, chans = direct_ref.shape[0], direct_ref.shape[1] // count
    rows = min(256, total)

    def body(block, _):
        base = pl.multiple_of(block * rows, rows)
        parts = []
        for m in range(count):
            wide = src_ref[m, pl.ds(base, rows), :]
            parts.append(wide[:, :chans] + wide[:, chans:])
        summed = jnp.concatenate(parts, axis=1) if count > 1 else parts[0]
        direct = direct_ref[pl.ds(base, rows), :].astype(f32)
        dst_ref[pl.ds(base, rows), :] = (summed + skip * direct).astype(bf16)
        return 0

    lax.fori_loop(0, total // rows, body, 0)


def scan_kernel(count, step, keep_ref, u_ref, par_ref, skip_ref, y_ref, u_wide, y_wide):
    total = u_ref.shape[0]
    turn_re, turn_im, res_re, res_im = (par_ref[i] for i in range(4))
    widen(u_ref, u_wide, count)

    def body(block, states):
        states = list(states)
        base = pl.multiple_of(block * step, step)
        for i in range(step):
            for m in range(count):
                x_re, x_im = states[m]
                keep = keep_ref[m, base + i]
                mul_re, mul_im = turn_re * keep, turn_im * keep
                new_re = mul_re * x_re + (u_wide[m, pl.ds(base + i, 1), :] - mul_im * x_im)
                new_im = mul_re * x_im + mul_im * x_re
                y_wide[m, pl.ds(base + i, 1), :] = jnp.sum(
                    res_re * new_re - res_im * new_im, axis=0, keepdims=True
                )
                states[m] = (new_re, new_im)
        return tuple(states)

    zero = jnp.zeros(turn_re.shape, f32)
    lax.fori_loop(0, total // step, body, tuple((zero, zero) for _ in range(count)))
    narrow(y_wide, u_ref, skip_ref[...], y_ref, count)


def back_kernel(
    count, step, keep_ref, u_ref, g_ref, par_ref, skip_ref, d_ref, sums_ref, skip_sum_ref, u_wide, g_wide, d_wide
):
    total = u_ref.shape[0]
    blocks = total // step
    turn_re, turn_im, res_re, res_im = (par_ref[i] for i in range(4))
    zero = jnp.zeros(turn_re.shape, f32)
    widen(u_ref, u_wide, count)
    widen(g_ref, g_wide, count)

    def body(block, carry):
        ahead, behind, sums = list(carry[0]), list(carry[1]), carry[2]
        base = pl.multiple_of(block * step, step)
        rear = pl.multiple_of((blocks - 1 - block) * step, step)
        for i in range(step):
            j = step - 1 - i
            for m in range(count):
                x_re, x_im, w_re, w_im = ahead[m]
                keep = keep_ref[m, base + i]
                mul_re, mul_im = turn_re * keep, turn_im * keep
                sum_re, sum_im = w_re + x_re, w_im + x_im
                w_re, w_im = mul_re * sum_re - mul_im * sum_im, mul_re * sum_im + mul_im * sum_re
                x_re, x_im = (
                    mul_re * x_re + (u_wide[m, pl.ds(base + i, 1), :] - mul_im * x_im),
                    mul_re * x_im + mul_im * x_re,
                )
                ahead[m] = (x_re, x_im, w_re, w_im)
                cot = g_wide[m, pl.ds(base + i, 1), :]
                sums = (
                    sums[0] + cot * x_re,
                    sums[1] + cot * x_im,
                    sums[2] + cot * w_re,
                    sums[3] + cot * w_im,
                )
                z_re, z_im, keep = behind[m]
                mul_re, mul_im = turn_re * keep, turn_im * keep
                z_re, z_im = (
                    mul_re * z_re + (g_wide[m, pl.ds(rear + j, 1), :] - mul_im * z_im),
                    mul_re * z_im + mul_im * z_re,
                )
                behind[m] = (z_re, z_im, keep_ref[m, rear + j])
                d_wide[m, pl.ds(rear + j, 1), :] = jnp.sum(res_re * z_re - res_im * z_im, axis=0, keepdims=True)
        return tuple(ahead), tuple(behind), sums

    start = (
        tuple((zero, zero, zero, zero) for _ in range(count)),
        tuple((zero, zero, jnp.float32(0)) for _ in range(count)),
        (zero, zero, zero, zero),
    )
    _, _, (g_re, g_im, lag_re, lag_im) = lax.fori_loop(0, blocks, body, start)
    sums_ref[0] = res_im * lag_im - res_re * lag_re
    sums_ref[1] = zero - (res_re * lag_im + res_im * lag_re)
    sums_ref[2] = g_re
    sums_ref[3] = zero - g_im
    narrow(d_wide, g_ref, skip_ref[...], d_ref, count)
    skip_sum_ref[...] = jnp.sum(u_ref[...].astype(f32) * g_ref[...].astype(f32), axis=0, keepdims=True)


def in_vmem():
    return pl.BlockSpec(memory_space=pltpu.VMEM)


def long_conv(u, keep, params, skips, count):
    total, width = u.shape
    return pl.pallas_call(
        functools.partial(scan_kernel, count, 16),
        out_shape=jax.ShapeDtypeStruct(u.shape, bf16),
        in_specs=[pl.BlockSpec(memory_space=pltpu.SMEM)] + [in_vmem()] * 3,
        out_specs=in_vmem(),
        scratch_shapes=[pltpu.VMEM((count, total, 2 * width // count), f32)] * 2,
        compiler_params=pltpu.CompilerParams(vmem_limit_bytes=48 << 20),
    )(keep, u, params, skips)


def long_conv_back(u, g, keep, params, skips, count):
    total, width = u.shape
    return pl.pallas_call(
        functools.partial(back_kernel, count, 16),
        out_shape=(
            jax.ShapeDtypeStruct(u.shape, bf16),
            jax.ShapeDtypeStruct(params.shape, f32),
            jax.ShapeDtypeStruct((1, width), f32),
        ),
        in_specs=[pl.BlockSpec(memory_space=pltpu.SMEM)] + [in_vmem()] * 4,
        out_specs=(in_vmem(),) * 3,
        scratch_shapes=[pltpu.VMEM((count, total, 2 * width // count), f32)] * 3,
        compiler_params=pltpu.CompilerParams(vmem_limit_bytes=48 << 20),
    )(keep, u, g, params, skips)


def pack_modes(rates, angles, res_re, res_im):
    def on_lanes(part):
        turned = part.T
        return jnp.concatenate([turned[:half_modes], turned[half_modes:]], axis=1)

    fading = jnp.exp(-rates)
    return jnp.stack(
        [on_lanes(part) for part in (fading * jnp.cos(angles), fading * jnp.sin(angles), res_re, res_im)]
    )


def shifted(array, axis, by):
    size = lax.axis_size(axis)
    pairs = [(i, i + by) for i in range(size) if 0 <= i + by < size]
    return lax.ppermute(array, axis, pairs)


def places_of(doc_lens, total):
    tokens = jnp.arange(total, dtype=jnp.int32)
    starts = jnp.cumsum(doc_lens, dtype=jnp.int32) - doc_lens
    begins = jnp.max(jnp.where(starts[None, :] <= tokens[:, None], starts[None, :], 0), axis=1)
    return tokens - begins


def dot_rows(left, right):
    return lax.dot_general(left, right, (((1,), (1,)), ((), ())), preferred_element_type=f32)


def dot_tokens(left, right):
    return lax.dot_general(left, right, (((0,), (0,)), ((), ())), preferred_element_type=f32)


def dot(left, right):
    return jnp.dot(left, right, preferred_element_type=f32)


def along_line(array, pairs):
    return lax.ppermute(array, "fsdp", pairs)


outer_pairs = [(0, 1), (1, 0), (2, 3), (3, 2)]
inner_pairs = [(1, 2), (2, 1)]


def gather_share(share):
    own = lax.axis_index("fsdp")
    next_one = along_line(share, outer_pairs)
    inner_one = along_line(share, inner_pairs)
    outer_two = along_line(inner_one, outer_pairs)
    inner_two = along_line(next_one, inner_pairs)
    outer_three = along_line(inner_two, outer_pairs)
    by_offset = (share, next_one, outer_two + inner_two, outer_three + inner_one)
    blocks = []
    for place in range(4):
        offset = own ^ place
        block = by_offset[3]
        for k in range(3):
            block = jnp.where(offset == k, by_offset[k], block)
        blocks.append(block)
    return lax.optimization_barrier(jnp.concatenate(blocks, axis=1))


def scatter_share(partial_sums):
    own = lax.axis_index("fsdp")
    share = partial_sums.shape[1] // 4

    def part(offset):
        return lax.dynamic_slice_in_dim(partial_sums, (own ^ offset) * share, share, 1)

    far = along_line(part(3).astype(bf16), outer_pairs)
    near = along_line(part(2).astype(bf16), outer_pairs)
    far = along_line((part(2) + far).astype(bf16), inner_pairs)
    near = along_line((part(3) + near).astype(bf16), inner_pairs)
    last = along_line((part(1) + far).astype(bf16), outer_pairs)
    return part(0).astype(f32) + last.astype(f32) + near.astype(f32)


def sum_line(array):
    array = array + along_line(array, outer_pairs)
    return array + along_line(array, [(i, i ^ 2) for i in range(4)])


def swap_seq(array, bit):
    return lax.ppermute(array, "seq", [(i, i ^ (1 << bit)) for i in range(lax.axis_size("seq"))])


def gather_weight(shard):
    return lax.all_gather(shard, "seq", axis=0, tiled=True)


def scatter_weight(grad):
    count = lax.axis_size("seq")
    rank = lax.axis_index("seq")
    bits = count.bit_length() - 1
    rows = grad.shape[0] // count

    def halve(array, left, bit):
        dim, mine = left.index(bit), (rank >> bit) & 1
        keep = lax.dynamic_index_in_dim(array, mine, dim, keepdims=False)
        give = lax.dynamic_index_in_dim(array, 1 - mine, dim, keepdims=False)
        got = swap_seq(give.astype(bf16), bit)
        return keep.astype(f32) + got.astype(f32), [other for other in left if other != bit]

    left = list(range(bits))[::-1]
    summed, left = halve(grad.reshape((2,) * bits + (rows, grad.shape[1])), left, 0)
    chip_bits = list(range(1, bits))
    middle = len(chip_bits) // 2
    parts = []
    for half, order in enumerate((chip_bits, chip_bits[middle:] + chip_bits[:middle])):
        part = lax.slice_in_dim(summed, half * rows // 2, (half + 1) * rows // 2, axis=summed.ndim - 2)
        rest = left
        for bit in order:
            part, rest = halve(part, rest, bit)
        parts.append(part)
    return jnp.concatenate(parts, axis=0)


def sum_seq(array):
    for bit in range(lax.axis_size("seq").bit_length() - 1):
        array = array + swap_seq(array, bit)
    return array


def to_channels(token_side, batches):
    rows, chans = token_side.shape[0] // batches, token_side.shape[1]
    count = lax.axis_size("seq")
    part = chans // count
    pieces = token_side.reshape(batches, rows, count, part).transpose(2, 1, 0, 3)
    sent = lax.all_to_all(pieces.reshape(count, rows, batches * part), "seq", split_axis=0, concat_axis=0)
    return sent.reshape(count * rows, batches * part)


def to_tokens(channel_side, batches):
    total, width = channel_side.shape
    count = lax.axis_size("seq")
    rows, part = total // count, width // batches
    sent = lax.all_to_all(channel_side.reshape(count, rows, width), "seq", split_axis=0, concat_axis=0)
    return sent.reshape(count, rows, batches, part).transpose(2, 1, 0, 3).reshape(batches * rows, count * part)


def on_device(
    hidden_in,
    out_cot,
    doc_lengths,
    mixer_gain,
    in_proj,
    short_filter,
    decay_rate,
    mode_angle,
    residue_re,
    residue_im,
    skip_gain,
    out_proj,
    feed_gain,
    gate_proj,
    up_proj,
    down_proj,
):
    batches, rows, share = hidden_in.shape
    tokens = batches * rows
    width = mixer_gain.shape[0]
    seq_count = lax.axis_size("seq")
    seq_rank = lax.axis_index("seq")
    fsdp_rank = lax.axis_index("fsdp")
    total = rows * seq_count
    chan_here = share // seq_count
    d_rows = in_proj.shape[0]

    x_share = hidden_in.reshape(tokens, share)
    cot_share = out_cot.reshape(tokens, share)
    x_all = gather_share(x_share).astype(f32)
    w_in = gather_weight(in_proj.reshape(d_rows, 3 * share))
    w_out = gather_weight(out_proj.T)
    units = gate_proj.shape[1]
    w_feed = gather_weight(jnp.concatenate([gate_proj, up_proj], axis=1))
    w_down = gather_weight(down_proj.T)

    places = jnp.stack([places_of(doc_lengths[m], total) for m in range(batches)])
    keep = (places > 0).astype(f32)
    places_here = lax.dynamic_slice_in_dim(places, seq_rank * rows, rows, 1)
    masks = [(places_here >= lag).astype(f32)[:, :, None] for lag in range(3)]
    taps = short_filter.reshape(3, 3 * share)

    def own_channels(part):
        return lax.dynamic_slice_in_dim(part, seq_rank * chan_here, chan_here, 0)

    modes = pack_modes(*(own_channels(part) for part in (decay_rate, mode_angle, residue_re, residue_im)))
    skips = jnp.tile(own_channels(skip_gain), batches)[None]

    scale_one = lax.rsqrt(jnp.mean(x_all * x_all, axis=-1, keepdims=True) + norm_eps)
    unit_one = x_all * scale_one
    normed_one = (unit_one * mixer_gain).astype(bf16)
    project = dot(normed_one, w_in).reshape(batches, rows, 3 * share)
    extended = jnp.concatenate([shifted(project[:, -2:], "seq", 1), project], axis=1)
    lagged = [extended[:, 2 - lag : 2 - lag + rows] for lag in range(3)]
    conv = sum(taps[lag] * masks[lag] * lagged[lag] for lag in range(3)).reshape(tokens, 3 * share)
    gate_one, gate_two, values = (conv[:, j * share : (j + 1) * share] for j in range(3))
    product = (gate_two * values).astype(bf16)
    product, cot_share = lax.optimization_barrier((product, cot_share))
    cot_all = gather_share(cot_share)
    channel_in = to_channels(product, batches)
    channel_out = long_conv(channel_in, keep, modes, skips, batches)
    mixed = to_tokens(channel_out, batches).astype(f32)
    gated = (gate_one * mixed).astype(bf16)
    stream = x_share.astype(f32) + scatter_share(dot_rows(gated, w_out).astype(bf16))
    stream_all = gather_share(stream.astype(bf16)).astype(f32)
    scale_two = lax.rsqrt(jnp.mean(stream_all * stream_all, axis=-1, keepdims=True) + norm_eps)
    unit_two = stream_all * scale_two
    normed_two = (unit_two * feed_gain).astype(bf16)
    feed_pre = dot(normed_two, w_feed)
    gate_pre, up_pre = feed_pre[:, :units], feed_pre[:, units:]
    sigmoid = jax.nn.sigmoid(gate_pre)
    activated = gate_pre * sigmoid
    hidden = (activated * up_pre).astype(bf16)
    down_part = dot_rows(hidden, w_down).astype(bf16)

    d_hidden = dot(cot_all, w_down)
    d_gate = d_hidden * up_pre * sigmoid * (1.0 + gate_pre * (1.0 - sigmoid))
    d_up = d_hidden * activated
    d_feed = jnp.concatenate([d_gate.astype(bf16), d_up.astype(bf16)], axis=1)
    part_two = dot_rows(d_feed, w_feed).astype(bf16)
    along_two = sum_line(jnp.sum(d_feed.astype(f32) * feed_pre, axis=-1).reshape(-1, 128)).reshape(tokens, 1)
    feed_gain_part = jnp.sum(unit_two * part_two.astype(f32), axis=0)

    def own_features(part):
        return lax.dynamic_slice_in_dim(part, fsdp_rank * share, share, 0)

    d_stream = (
        cot_share.astype(f32)
        + scale_two * own_features(feed_gain) * scatter_share(part_two)
        - stream * (scale_two * scale_two * along_two / width)
    )
    d_mix = gather_share(d_stream.astype(bf16))
    grad_down = dot_tokens(cot_all, hidden).astype(bf16)
    grad_feed = dot_tokens(normed_two, d_feed).astype(bf16)
    down_grad = scatter_weight(grad_down).T
    feed_grad = scatter_weight(grad_feed)

    d_gated = dot(d_mix, w_out)
    d_gated, down_part = lax.optimization_barrier((d_gated, down_part))
    block_out = stream + scatter_share(down_part)
    out_grad = scatter_weight(dot_tokens(d_mix, gated).astype(bf16)).T
    d_gate_one = d_gated * mixed
    back_in = to_channels((d_gated * gate_one).astype(bf16), batches)
    back_out, mode_sums, skip_sums = long_conv_back(channel_in, back_in, keep, modes, skips, batches)
    d_product = to_tokens(back_out, batches).astype(f32)
    d_conv = jnp.concatenate([d_gate_one, d_product * values, d_product * gate_two], axis=1)
    d_conv = d_conv.reshape(batches, rows, 3 * share)
    short_part = jnp.stack([jnp.sum(masks[lag] * lagged[lag] * d_conv, axis=(0, 1)) for lag in range(3)])
    spread = sum(
        jnp.pad(taps[lag] * masks[lag] * d_conv, ((0, 0), (2 - lag, lag), (0, 0))) for lag in range(3)
    )
    returned = shifted(spread[:, :2], "seq", -1)
    d_project = spread[:, 2:] + jnp.pad(returned, ((0, 0), (rows - 2, 0), (0, 0)))
    d_project = d_project.astype(bf16).reshape(tokens, 3 * share)
    along_one = jnp.sum(d_project.astype(f32) * project.reshape(tokens, 3 * share), axis=-1)
    along_one = sum_line(along_one.reshape(-1, 128)).reshape(tokens, 1)
    part_one = dot_rows(d_project, w_in).astype(bf16)
    mixer_gain_part = jnp.sum(unit_one * part_one.astype(f32), axis=0)
    d_x = (
        d_stream
        + scale_one * own_features(mixer_gain) * scatter_share(part_one)
        - x_share.astype(f32) * (scale_one * scale_one * along_one / width)
    )

    in_grad = scatter_weight(dot_tokens(normed_one, d_project).astype(bf16)).reshape(d_rows, 3, share)
    gains = sum_seq(sum_line(jnp.concatenate([mixer_gain_part, feed_gain_part]).reshape(-1, 128)))
    gains = gains.reshape(2, width)
    short_grad = sum_seq(short_part).reshape(3, 3, share)
    skip_own = jnp.sum(skip_sums.reshape(batches, chan_here), axis=0)
    skip_rows = jnp.zeros((half_modes, 2 * chan_here), f32).at[0, :chan_here].set(skip_own)
    filters = jnp.concatenate([mode_sums, skip_rows[None]], axis=0)
    filters = lax.all_gather(filters, "seq", axis=0)
    by_chan = filters.reshape(seq_count, 5, half_modes, 2, chan_here).transpose(1, 0, 4, 3, 2)
    by_chan = by_chan.reshape(5, share, 2 * half_modes)
    return (
        block_out.astype(bf16).reshape(hidden_in.shape),
        d_x.reshape(hidden_in.shape),
        gains[0],
        in_grad,
        short_grad,
        by_chan[0],
        by_chan[1],
        by_chan[2],
        by_chan[3],
        by_chan[4, :, 0],
        out_grad,
        gains[1],
        feed_grad[:, :units],
        feed_grad[:, units:],
        down_grad,
    )


def solution(mesh):
    tokens = P(None, "seq", "fsdp")
    chan_rows = P("fsdp", None)
    d_rows = P("seq", "fsdp")
    d_cols = P("fsdp", "seq")
    in_specs = (
        tokens,
        tokens,
        P(),
        P(),
        P("seq", None, "fsdp"),
        P(None, None, "fsdp"),
        chan_rows,
        chan_rows,
        chan_rows,
        chan_rows,
        P("fsdp"),
        d_cols,
        P(),
        d_rows,
        d_rows,
        d_cols,
    )
    out_specs = (
        tokens,
        tokens,
        P(),
        P("seq", None, "fsdp"),
        P(None, None, "fsdp"),
        chan_rows,
        chan_rows,
        chan_rows,
        chan_rows,
        P("fsdp"),
        d_cols,
        P(),
        d_rows,
        d_rows,
        d_cols,
    )
    return jax.shard_map(on_device, mesh=mesh, in_specs=in_specs, out_specs=out_specs, check_vma=False)
```

```python
import functools

import jax
import jax.numpy as jnp
from jax import lax
from jax.experimental import pallas as pl
from jax.experimental.pallas import tpu as pltpu
from jax.sharding import PartitionSpec as P

norm_eps = 1e-05
half_modes = 8
f32 = jnp.float32
bf16 = jnp.bfloat16


lane_block = 128
step = 8


def times(a_re, a_im, b_re, b_im):
    return a_re * b_re - a_im * b_im, a_re * b_im + a_im * b_re


def each_block(width, body):
    def run(block, carry):
        body(block, pl.ds(pl.multiple_of(block * lane_block, lane_block), lane_block))
        return carry

    lax.fori_loop(0, width // lane_block, run, 0)


def widen(src_ref, dst_ref):
    for block in range(dst_ref.shape[0]):
        dst_ref[block] = src_ref[:, block * lane_block : (block + 1) * lane_block].astype(f32)


def narrow(src_ref, direct_ref, skip_ref, dst_ref):
    for block in range(src_ref.shape[0]):
        lanes = slice(block * lane_block, (block + 1) * lane_block)
        dst_ref[:, lanes] = (src_ref[block] + skip_ref[:, lanes] * direct_ref[block]).astype(bf16)


def load_pairs(ref, index, lanes):
    return [(ref[index, h, :, lanes], ref[index + 1, h, :, lanes]) for h in range(2)]


def edge_kernel(batches, reverse, keep_ref, u_ref, par_ref, edge_ref, u_wide):
    tokens, share = u_ref.shape
    rows = tokens // batches
    widen(u_ref, u_wide)

    def on_lanes(at, lanes):
        turn = load_pairs(par_ref, 0, lanes)

        def body(block, states):
            states = [list(own) for own in states]
            for i in range(step):
                t = block * step + i
                t = rows - 1 - t if reverse else t
                for m in range(batches):
                    keep = keep_ref[m, t]
                    row = u_wide[at, pl.ds(m * rows + t, 1), :]
                    for h in range(2):
                        re, im = states[m][h]
                        turn_re, turn_im = turn[h][0] * keep, turn[h][1] * keep
                        if reverse:
                            states[m][h] = times(turn_re, turn_im, re + row, im)
                        else:
                            re, im = times(turn_re, turn_im, re, im)
                            states[m][h] = (re + row, im)
            return tuple(tuple(own) for own in states)

        zero = jnp.zeros((half_modes, lane_block), f32)
        states = lax.fori_loop(0, rows // step, body, (((zero, zero),) * 2,) * batches)
        for m in range(batches):
            for h in range(2):
                edge_ref[m, 0, h, :, lanes], edge_ref[m, 1, h, :, lanes] = states[m][h]

    each_block(share, on_lanes)


def load_states(ref, batches, lanes):
    return tuple(
        tuple((ref[m, 0, h, :, lanes], ref[m, 1, h, :, lanes]) for h in range(2)) for m in range(batches)
    )


def conv_kernel(batches, keep_ref, u_ref, into_ref, par_ref, skip_ref, y_ref, u_wide, y_wide):
    tokens, share = u_ref.shape
    rows = tokens // batches
    widen(u_ref, u_wide)

    def on_lanes(at, lanes):
        turn, res = (load_pairs(par_ref, 2 * i, lanes) for i in range(2))

        def body(block, states):
            states = [list(own) for own in states]
            for i in range(step):
                t = block * step + i
                for m in range(batches):
                    keep = keep_ref[m, t]
                    row = u_wide[at, pl.ds(m * rows + t, 1), :]
                    out = []
                    for h in range(2):
                        re, im = times(turn[h][0] * keep, turn[h][1] * keep, *states[m][h])
                        re = re + row
                        states[m][h] = (re, im)
                        out.append(res[h][0] * re - res[h][1] * im)
                    y_wide[at, pl.ds(m * rows + t, 1), :] = jnp.sum(out[0] + out[1], axis=0, keepdims=True)
            return tuple(tuple(own) for own in states)

        lax.fori_loop(0, rows // step, body, load_states(into_ref, batches, lanes))

    each_block(share, on_lanes)
    narrow(y_wide, u_wide, skip_ref, y_ref)


def back_kernel(
    batches,
    keep_ref,
    u_ref,
    g_ref,
    into_ref,
    behind_ref,
    par_ref,
    skip_ref,
    d_ref,
    sums_ref,
    skip_sum_ref,
    u_wide,
    g_wide,
    d_wide,
    kept,
):
    tokens, share = u_ref.shape
    rows = tokens // batches
    widen(u_ref, u_wide)
    widen(g_ref, g_wide)

    def on_lanes(at, lanes):
        turn, res = (load_pairs(par_ref, 2 * i, lanes) for i in range(2))

        def ahead(block, states):
            states = [list(own) for own in states]
            for i in range(step):
                t = block * step + i
                for m in range(batches):
                    keep = keep_ref[m, t]
                    row = u_wide[at, pl.ds(m * rows + t, 1), :]
                    for h in range(2):
                        re, im = times(turn[h][0] * keep, turn[h][1] * keep, *states[m][h])
                        kept[t, m, h, 0], kept[t, m, h, 1] = re, im
                        states[m][h] = (re + row, im)
            return tuple(tuple(own) for own in states)

        lax.fori_loop(0, rows // step, ahead, load_states(into_ref, batches, lanes))
        start = load_states(behind_ref, batches, lanes)

        def behind(block, carry):
            states, sums = [list(own) for own in carry[0]], list(carry[1])
            for i in range(step):
                t = rows - 1 - (block * step + i)
                for m in range(batches):
                    keep = keep_ref[m, t]
                    row = g_wide[at, pl.ds(m * rows + t, 1), :]
                    out = []
                    for h in range(2):
                        re, im = states[m][h]
                        re = re + row
                        x_re, x_im = kept[t, m, h, 0], kept[t, m, h, 1]
                        lag_re, lag_im = times(re, im, x_re, x_im)
                        g_re, g_im, w_re, w_im = sums[h]
                        sums[h] = (g_re + row * x_re, g_im + row * x_im, w_re + lag_re, w_im + lag_im)
                        out.append(res[h][0] * re - res[h][1] * im)
                        states[m][h] = times(turn[h][0] * keep, turn[h][1] * keep, re, im)
                    d_wide[at, pl.ds(m * rows + t, 1), :] = jnp.sum(out[0] + out[1], axis=0, keepdims=True)
            return tuple(tuple(own) for own in states), tuple(sums)

        zero = jnp.zeros((half_modes, lane_block), f32)
        skip_sum = jnp.sum(u_wide[at] * g_wide[at], axis=0, keepdims=True)
        skip_sum_ref[:, lanes] = skip_sum
        _, sums = lax.fori_loop(0, rows // step, behind, (start, ((zero,) * 4,) * 2))
        for h in range(2):
            g_re, g_im, w_re, w_im = sums[h]
            lag_re, lag_im = times(*res[h], w_re, w_im)
            sums_ref[0, h, :, lanes] = zero - lag_re
            sums_ref[1, h, :, lanes] = zero - lag_im
            sums_ref[2, h, :, lanes] = g_re + skip_sum
            sums_ref[3, h, :, lanes] = zero - g_im

    each_block(share, on_lanes)
    narrow(d_wide, g_wide, skip_ref, d_ref)


def in_vmem():
    return pl.BlockSpec(memory_space=pltpu.VMEM)


def in_smem():
    return pl.BlockSpec(memory_space=pltpu.SMEM)


def scratch_rows(u):
    return pltpu.VMEM((u.shape[1] // lane_block, u.shape[0], lane_block), f32)


def edge_states(u, keep, params, reverse):
    batches = keep.shape[0]
    return pl.pallas_call(
        functools.partial(edge_kernel, batches, reverse),
        out_shape=jax.ShapeDtypeStruct((batches, 2) + params.shape[1:], f32),
        in_specs=[in_smem(), in_vmem(), in_vmem()],
        out_specs=in_vmem(),
        scratch_shapes=[scratch_rows(u)],
        compiler_params=pltpu.CompilerParams(vmem_limit_bytes=48 << 20),
    )(keep, u, params)


def long_conv(keep, u, into, params, skips):
    return pl.pallas_call(
        functools.partial(conv_kernel, keep.shape[0]),
        out_shape=jax.ShapeDtypeStruct(u.shape, bf16),
        in_specs=[in_smem()] + [in_vmem()] * 4,
        out_specs=in_vmem(),
        scratch_shapes=[scratch_rows(u)] * 2,
        compiler_params=pltpu.CompilerParams(vmem_limit_bytes=48 << 20),
    )(keep, u, into, params, skips)


def long_conv_back(keep, u, g, into, behind, params, skips):
    batches, rows = keep.shape
    return pl.pallas_call(
        functools.partial(back_kernel, batches),
        out_shape=(
            jax.ShapeDtypeStruct(u.shape, bf16),
            jax.ShapeDtypeStruct((4,) + params.shape[1:], f32),
            jax.ShapeDtypeStruct((1, u.shape[1]), f32),
        ),
        in_specs=[in_smem()] + [in_vmem()] * 6,
        out_specs=(in_vmem(),) * 3,
        scratch_shapes=[scratch_rows(u)] * 3 + [pltpu.VMEM((rows, batches, 2, 2, half_modes, lane_block), f32)],
        compiler_params=pltpu.CompilerParams(vmem_limit_bytes=48 << 20),
    )(keep, u, g, into, behind, params, skips)


def shifted(array, axis, by):
    size = lax.axis_size(axis)
    pairs = [(i, i + by) for i in range(size) if 0 <= i + by < size]
    return lax.ppermute(array, axis, pairs)


def places_of(doc_lens, total):
    tokens = jnp.arange(total, dtype=jnp.int32)
    starts = jnp.cumsum(doc_lens, dtype=jnp.int32) - doc_lens
    begins = jnp.max(jnp.where(starts[None, :] <= tokens[:, None], starts[None, :], 0), axis=1)
    return tokens - begins


def dot_rows(left, right):
    return lax.dot_general(left, right, (((1,), (1,)), ((), ())), preferred_element_type=f32)


def dot_tokens(left, right):
    return lax.dot_general(left, right, (((0,), (0,)), ((), ())), preferred_element_type=f32)


def dot(left, right):
    return jnp.dot(left, right, preferred_element_type=f32)


def along_line(array, pairs):
    return lax.ppermute(array, "fsdp", pairs)


outer_pairs = [(0, 1), (1, 0), (2, 3), (3, 2)]
inner_pairs = [(1, 2), (2, 1)]


def after(value, *others):
    return lax.optimization_barrier((value,) + others)[0]


def gather_first(share):
    return along_line(share, outer_pairs), along_line(share, inner_pairs)


def gather_second(first):
    next_one, inner_one = first
    return along_line(inner_one, outer_pairs), along_line(next_one, inner_pairs)


def gather_last(second):
    return along_line(second[1], outer_pairs)


def gathered(share, first, second, last):
    own = lax.axis_index("fsdp")
    by_offset = (share, first[0], second[0] + second[1], last + first[1])
    blocks = []
    for place in range(4):
        offset = own ^ place
        block = by_offset[3]
        for k in range(3):
            block = jnp.where(offset == k, by_offset[k], block)
        blocks.append(block)
    return lax.optimization_barrier(jnp.concatenate(blocks, axis=1))


def gather_share(share):
    first = gather_first(share)
    second = gather_second(first)
    return gathered(share, first, second, gather_last(second))


def part_of(partial_sums, offset):
    share = partial_sums.shape[1] // 4
    return lax.dynamic_slice_in_dim(partial_sums, (lax.axis_index("fsdp") ^ offset) * share, share, 1)


def scatter_first(partial_sums):
    return along_line(part_of(partial_sums, 3), outer_pairs), along_line(part_of(partial_sums, 2), outer_pairs)


def scatter_second(partial_sums, first):
    far, near = first
    return (
        along_line(part_of(partial_sums, 2) + far, inner_pairs),
        along_line(part_of(partial_sums, 3) + near, inner_pairs),
    )


def scatter_last(partial_sums, second):
    return along_line(part_of(partial_sums, 1) + second[0], outer_pairs)


def scattered(partial_sums, second, last):
    return part_of(partial_sums, 0).astype(f32) + last.astype(f32) + second[1].astype(f32)


def scatter_offloaded(partial_sums):
    return lax.psum_scatter(partial_sums, "fsdp", scatter_dimension=1, tiled=True).astype(f32)


def sum_line(array):
    array = array + along_line(array, outer_pairs)
    return array + along_line(array, [(i, i ^ 2) for i in range(4)])


def swap_seq(array, bit):
    return lax.ppermute(array, "seq", [(i, i ^ (1 << bit)) for i in range(lax.axis_size("seq"))])


def gather_weight(shard):
    return lax.all_gather(shard, "seq", axis=0, tiled=True)


def of_core(left, core):
    count = lax.axis_size("seq")
    rows = left.shape[1] // count
    parts = [lax.dynamic_slice_in_dim(left, (2 * chip + core) * rows, rows, 1) for chip in range(count // 2)]
    return lax.optimization_barrier(jnp.concatenate(parts, axis=1))


def core_give(left, right):
    core = lax.axis_index("seq") % 2
    return lax.optimization_barrier(dot_tokens(of_core(left, 1 - core), right).astype(bf16))


def core_sum(left, right, got):
    own = dot_tokens(of_core(left, lax.axis_index("seq") % 2), right)
    return lax.optimization_barrier((own + got.astype(f32)).astype(bf16))


def chip_sums_offloaded(summed):
    count = lax.axis_size("seq")
    groups = [list(range(core, count, 2)) for core in range(2)]
    return lax.psum_scatter(summed, "seq", scatter_dimension=0, axis_index_groups=groups, tiled=True).astype(f32)


def chip_sums(summed):
    count = lax.axis_size("seq")
    rank = lax.axis_index("seq")
    rows, bits = 2 * summed.shape[0] // count, count.bit_length() - 1
    by_bits = summed.reshape((2,) * (bits - 1) + (rows, summed.shape[1]))

    def halve(array, rest, bit):
        dim, mine = rest.index(bit), (rank >> bit) & 1
        keep = lax.dynamic_index_in_dim(array, mine, dim, keepdims=False)
        give = lax.dynamic_index_in_dim(array, 1 - mine, dim, keepdims=False)
        got = swap_seq(give.astype(bf16), bit)
        return keep.astype(f32) + got.astype(f32), [other for other in rest if other != bit]

    chip_bits = list(range(1, bits))
    middle = len(chip_bits) // 2
    parts = []
    for half, order in enumerate((chip_bits, chip_bits[middle:] + chip_bits[:middle])):
        part = lax.slice_in_dim(by_bits, half * rows // 2, (half + 1) * rows // 2, axis=bits - 1)
        rest = chip_bits[::-1]
        for bit in order:
            part, rest = halve(part, rest, bit)
        parts.append(part)
    return lax.optimization_barrier(jnp.concatenate(parts, axis=0))


def passing_factors(whole, power, reverse):
    count = lax.axis_size("seq")
    rank = lax.axis_index("seq")
    if reverse:
        rank, whole = count - 1 - rank, whole[:, ::-1]
    devices = jnp.arange(count)

    def factor(exponent, within):
        kept = jnp.min(jnp.where(within, whole, 1.0), axis=1)[:, None, None, None]
        return jnp.stack([part * kept for part in power(exponent)])

    steps = []
    for bit in range(count.bit_length() - 1):
        size = 1 << bit
        group = rank // size
        later = (group % 2).astype(f32)
        ahead = factor((rank % size).astype(f32), (devices // size == group) & (devices < rank)) * later
        last = factor(float(size), devices // size == (group | 1))
        steps.append((ahead, last))
    return lax.optimization_barrier(steps)


def through(edge, factors, reverse):
    count = lax.axis_size("seq")
    rank = lax.axis_index("seq")
    if reverse:
        rank = count - 1 - rank

    def grown(factor, state):
        re, im = times(factor[0], factor[1], state[:, 0], state[:, 1])
        return jnp.stack([re, im], axis=1)

    into = jnp.zeros_like(edge)
    for bit, (ahead, last) in enumerate(factors):
        later = (rank >> bit) & 1 == 1
        got = swap_seq(edge, bit)
        into = into + grown(ahead, got)
        if bit + 1 < len(factors):
            edge = jnp.where(later, edge, got) + grown(last, jnp.where(later, got, edge))
    return into


def sum_seq(array):
    for bit in range(lax.axis_size("seq").bit_length() - 1):
        array = array + swap_seq(array, bit)
    return array


def on_device(
    hidden_in,
    out_cot,
    doc_lengths,
    mixer_gain,
    in_proj,
    short_filter,
    decay_rate,
    mode_angle,
    residue_re,
    residue_im,
    skip_gain,
    out_proj,
    feed_gain,
    gate_proj,
    up_proj,
    down_proj,
):
    batches, rows, share = hidden_in.shape
    tokens = batches * rows
    width = mixer_gain.shape[0]
    seq_count = lax.axis_size("seq")
    seq_rank = lax.axis_index("seq")
    fsdp_rank = lax.axis_index("fsdp")
    total = rows * seq_count
    d_rows = in_proj.shape[0]

    x_share = hidden_in.reshape(tokens, share)
    cot_share = out_cot.reshape(tokens, share)
    x_all = gather_share(x_share).astype(f32)
    units = gate_proj.shape[1]
    w_in = gather_weight(in_proj.reshape(d_rows, 3 * share))
    w_both = gather_weight(jnp.concatenate([out_proj.T, down_proj.T], axis=1))
    w_out, w_down = w_both[:, :share], w_both[:, share:]
    w_feed = gather_weight(jnp.concatenate([gate_proj, up_proj], axis=1))

    places = jnp.stack([places_of(doc_lengths[m], total) for m in range(batches)])
    keep = (places > 0).astype(f32)
    places_here = lax.dynamic_slice_in_dim(places, seq_rank * rows, rows, 1)
    masks = [(places_here >= lag).astype(f32)[:, :, None] for lag in range(3)]
    taps = short_filter.reshape(3, 3 * share)

    keep_here = lax.dynamic_slice_in_dim(keep, seq_rank * rows, rows, 1)
    whole = jnp.min(keep.reshape(batches, seq_count, rows), axis=2)
    rates, angles, res_re, res_im = (
        part.T.reshape(2, half_modes, share) for part in (decay_rate, mode_angle, residue_re, residue_im)
    )

    def power(devices):
        fading = jnp.exp(-(devices * rows) * rates)
        return fading * jnp.cos((devices * rows) * angles), fading * jnp.sin((devices * rows) * angles)

    fading = jnp.exp(-rates)
    modes = jnp.stack([fading * jnp.cos(angles), fading * jnp.sin(angles), res_re, res_im])
    skips = skip_gain[None]
    factors = passing_factors(whole, power, False)
    back_factors = passing_factors(whole, power, True)

    scale_one = lax.rsqrt(jnp.mean(x_all * x_all, axis=-1, keepdims=True) + norm_eps)
    unit_one = x_all * scale_one
    normed_one = after((unit_one * mixer_gain).astype(bf16), modes, factors, back_factors)
    project = dot(normed_one, w_in).reshape(batches, rows, 3 * share)
    extended = jnp.concatenate([shifted(project[:, -2:], "seq", 1), project], axis=1)
    lagged = [extended[:, 2 - lag : 2 - lag + rows] for lag in range(3)]
    conv = sum(taps[lag] * masks[lag] * lagged[lag] for lag in range(3)).reshape(tokens, 3 * share)
    gate_one, gate_two, values = (conv[:, j * share : (j + 1) * share] for j in range(3))
    product = (gate_two * values).astype(bf16)
    cot_late = after(cot_share, product)
    cot_first = gather_first(cot_late)
    into = through(edge_states(product, keep_here, modes, False), factors, False)
    cot_second = gather_second(cot_first)
    mixed = long_conv(keep_here, product, after(into, *cot_first), modes, skips)
    cot_last = gather_last(cot_second)
    mixed = after(mixed, *cot_second).astype(f32)
    gated = (gate_one * mixed).astype(bf16)
    mix_part = dot_rows(gated, w_out).astype(bf16)
    mix_first = scatter_first(mix_part)
    mix_second = scatter_second(mix_part, mix_first)
    cot_all = gathered(cot_share, cot_first, cot_second, after(cot_last, mix_first[0]))
    d_hidden = lax.optimization_barrier(dot(cot_all, w_down))
    mix_last = scatter_last(mix_part, mix_second)
    stream = x_share.astype(f32) + scattered(mix_part, mix_second, mix_last)
    stream_all = gather_share(stream.astype(bf16)).astype(f32)
    scale_two = lax.rsqrt(jnp.mean(stream_all * stream_all, axis=-1, keepdims=True) + norm_eps)
    unit_two = stream_all * scale_two
    normed_two = lax.optimization_barrier((unit_two * feed_gain).astype(bf16))
    feed_pre = dot(normed_two, w_feed)
    gate_pre, up_pre = feed_pre[:, :units], feed_pre[:, units:]
    sigmoid = jax.nn.sigmoid(gate_pre)
    activated = gate_pre * sigmoid
    hidden = (activated * up_pre).astype(bf16)

    d_gate = d_hidden * up_pre * sigmoid * (1.0 + gate_pre * (1.0 - sigmoid))
    d_up = d_hidden * activated
    d_feed = jnp.concatenate([d_gate.astype(bf16), d_up.astype(bf16)], axis=1)
    part_two = dot_rows(d_feed, w_feed).astype(bf16)
    two_first = scatter_first(part_two)
    along_two = jnp.sum(after(d_feed, part_two).astype(f32) * feed_pre, axis=-1)
    along_two = sum_line(along_two.reshape(-1, 128)).reshape(tokens, 1)
    feed_gain_part = jnp.sum(unit_two * after(part_two, two_first[0]).astype(f32), axis=0)
    down_got = swap_seq(core_give(cot_all, after(hidden, part_two)), 0)
    two_second = scatter_second(part_two, two_first)
    feed_got = swap_seq(core_give(normed_two, after(d_feed, two_first[0])), 0)
    two_last = scatter_last(part_two, two_second)
    down_sum = core_sum(cot_all, hidden, after(down_got, two_second[0]))

    def own_features(part):
        return lax.dynamic_slice_in_dim(part, fsdp_rank * share, share, 0)

    d_stream = (
        cot_share.astype(f32)
        + scale_two * own_features(feed_gain) * scattered(part_two, two_second, two_last)
        - stream * (scale_two * scale_two * along_two / width)
    )
    d_share = d_stream.astype(bf16)
    mix_one = gather_first(d_share)
    mix_two = gather_second(mix_one)
    down_grad = chip_sums_offloaded(down_sum)
    down_part = dot_rows(after(hidden, d_share), w_down).astype(bf16)
    feed_sum = core_sum(normed_two, d_feed, after(feed_got, mix_one[0]))
    feed_grad = chip_sums_offloaded(feed_sum)
    mix_three = gather_last(after(mix_two, feed_sum, down_part, feed_gain_part))
    d_mix = gathered(d_share, mix_one, mix_two, mix_three)

    d_gated = lax.optimization_barrier(dot(d_mix, w_out))
    down_first = scatter_first(after(down_part, d_gated))
    d_gate_one = d_gated * mixed
    d_mixed = (d_gated * gate_one).astype(bf16)
    behind = through(edge_states(d_mixed, keep_here, modes, True), back_factors, True)
    down_second = scatter_second(down_part, down_first)
    out_sum = core_sum(d_mix, gated, swap_seq(core_give(d_mix, after(gated, d_mixed)), 0))
    down_last = scatter_last(down_part, down_second)
    out_grad = chip_sums_offloaded(out_sum)
    d_product, mode_sums, skip_sums = long_conv_back(
        keep_here, product, d_mixed, into, after(behind, *down_second), modes, skips
    )
    d_product = after(d_product, out_sum, down_last)
    block_out = stream + scattered(down_part, down_second, down_last)
    d_product = d_product.astype(f32)
    d_conv = jnp.concatenate([d_gate_one, d_product * values, d_product * gate_two], axis=1)
    d_conv = d_conv.reshape(batches, rows, 3 * share)
    short_part = jnp.stack([jnp.sum(masks[lag] * lagged[lag] * d_conv, axis=(0, 1)) for lag in range(3)])
    spread = sum(
        jnp.pad(taps[lag] * masks[lag] * d_conv, ((0, 0), (2 - lag, lag), (0, 0))) for lag in range(3)
    )
    returned = shifted(spread[:, :2], "seq", -1)
    d_project = spread[:, 2:] + jnp.pad(returned, ((0, 0), (rows - 2, 0), (0, 0)))
    d_project = d_project.astype(bf16).reshape(tokens, 3 * share)
    along_one = jnp.sum(d_project.astype(f32) * project.reshape(tokens, 3 * share), axis=-1)
    along_one = sum_line(along_one.reshape(-1, 128)).reshape(tokens, 1)
    part_one = dot_rows(d_project, w_in).astype(bf16)
    mixer_gain_part = jnp.sum(unit_one * part_one.astype(f32), axis=0)
    one_first = scatter_first(part_one)
    in_got = swap_seq(core_give(normed_one, after(d_project, part_one)), 0)
    one_second = scatter_second(part_one, one_first)
    in_sum = core_sum(normed_one, d_project, in_got)
    one_last = scatter_last(part_one, after(one_second, in_sum))
    d_x = (
        d_stream
        + scale_one * own_features(mixer_gain) * scattered(part_one, one_second, one_last)
        - x_share.astype(f32) * (scale_one * scale_one * along_one / width)
    )

    in_grad = chip_sums_offloaded(in_sum).reshape(d_rows, 3, share)
    small = [mixer_gain_part, feed_gain_part, short_part, mode_sums, skip_sums]
    small = sum_seq(jnp.concatenate([part.reshape(-1, 128) for part in small]))
    gains = sum_line(small[: 2 * width // 128]).reshape(2, width)
    small = small[2 * width // 128 :].reshape(-1, share)
    short_grad = small[:9].reshape(3, 3, share)
    filters = small[9:]
    by_chan = filters[:-1].reshape(4, 2 * half_modes, share).transpose(0, 2, 1)
    return (
        block_out.astype(bf16).reshape(hidden_in.shape),
        d_x.reshape(hidden_in.shape),
        gains[0],
        in_grad,
        short_grad,
        by_chan[0],
        by_chan[1],
        by_chan[2],
        by_chan[3],
        filters[-1],
        out_grad.T,
        gains[1],
        feed_grad[:, :units],
        feed_grad[:, units:],
        down_grad.T,
    )


def solution(mesh):
    tokens = P(None, "seq", "fsdp")
    chan_rows = P("fsdp", None)
    d_rows = P("seq", "fsdp")
    d_cols = P("fsdp", "seq")
    in_specs = (
        tokens,
        tokens,
        P(),
        P(),
        P("seq", None, "fsdp"),
        P(None, None, "fsdp"),
        chan_rows,
        chan_rows,
        chan_rows,
        chan_rows,
        P("fsdp"),
        d_cols,
        P(),
        d_rows,
        d_rows,
        d_cols,
    )
    out_specs = (
        tokens,
        tokens,
        P(),
        P("seq", None, "fsdp"),
        P(None, None, "fsdp"),
        chan_rows,
        chan_rows,
        chan_rows,
        chan_rows,
        P("fsdp"),
        d_cols,
        P(),
        d_rows,
        d_rows,
        d_cols,
    )
    return jax.shard_map(on_device, mesh=mesh, in_specs=in_specs, out_specs=out_specs, check_vma=False)
```

```python
import functools

import jax
import jax.numpy as jnp
from jax import lax
from jax.experimental import pallas as pl
from jax.experimental.pallas import tpu as pltpu
from jax.experimental.layout import Layout, with_layout_constraint
from jax.sharding import PartitionSpec as P

norm_eps = 1e-05
half_modes = 8
f32 = jnp.float32
bf16 = jnp.bfloat16


lane_block = 128
step = 16


def times(a_re, a_im, b_re, b_im):
    return a_re * b_re - a_im * b_im, a_re * b_im + a_im * b_re


def each_block(width, body):
    def run(block, carry):
        body(block, pl.ds(pl.multiple_of(block * lane_block, lane_block), lane_block))
        return carry

    lax.fori_loop(0, width // lane_block, run, 0)


def widen(src_ref, dst_ref):
    for block in range(dst_ref.shape[0]):
        dst_ref[block] = src_ref[:, block * lane_block : (block + 1) * lane_block].astype(f32)


def narrow(src_ref, direct_ref, skip_ref, dst_ref):
    for block in range(src_ref.shape[0]):
        lanes = slice(block * lane_block, (block + 1) * lane_block)
        dst_ref[:, lanes] = (src_ref[block] + skip_ref[:, lanes] * direct_ref[block]).astype(bf16)


def load_pairs(ref, index, lanes):
    return [(ref[index, h, :, lanes], ref[index + 1, h, :, lanes]) for h in range(2)]


def edge_kernel(batches, reverse, keep_ref, u_ref, par_ref, edge_ref, u_wide):
    tokens, share = u_ref.shape
    rows = tokens // batches
    widen(u_ref, u_wide)

    def on_lanes(at, lanes):
        turn = load_pairs(par_ref, 0, lanes)

        def body(block, states):
            states = [list(own) for own in states]
            for i in range(step):
                t = block * step + i
                t = rows - 1 - t if reverse else t
                for m in range(batches):
                    keep = keep_ref[m, t]
                    row = u_wide[at, pl.ds(m * rows + t, 1), :]
                    for h in range(2):
                        re, im = states[m][h]
                        turn_re, turn_im = turn[h][0] * keep, turn[h][1] * keep
                        if reverse:
                            states[m][h] = times(turn_re, turn_im, re + row, im)
                        else:
                            re, im = times(turn_re, turn_im, re, im)
                            states[m][h] = (re + row, im)
            return tuple(tuple(own) for own in states)

        zero = jnp.zeros((half_modes, lane_block), f32)
        states = lax.fori_loop(0, rows // step, body, (((zero, zero),) * 2,) * batches)
        for m in range(batches):
            for h in range(2):
                edge_ref[m, 0, h, :, lanes], edge_ref[m, 1, h, :, lanes] = states[m][h]

    each_block(share, on_lanes)


def load_states(ref, batches, lanes):
    return tuple(
        tuple((ref[m, 0, h, :, lanes], ref[m, 1, h, :, lanes]) for h in range(2)) for m in range(batches)
    )


def conv_kernel(batches, keep_ref, u_ref, into_ref, par_ref, skip_ref, y_ref, u_wide, y_wide):
    tokens, share = u_ref.shape
    rows = tokens // batches
    widen(u_ref, u_wide)

    def on_lanes(at, lanes):
        turn, res = (load_pairs(par_ref, 2 * i, lanes) for i in range(2))

        def body(block, states):
            states = [list(own) for own in states]
            for i in range(step):
                t = block * step + i
                for m in range(batches):
                    keep = keep_ref[m, t]
                    row = u_wide[at, pl.ds(m * rows + t, 1), :]
                    out = []
                    for h in range(2):
                        re, im = times(turn[h][0] * keep, turn[h][1] * keep, *states[m][h])
                        re = re + row
                        states[m][h] = (re, im)
                        out.append(res[h][0] * re - res[h][1] * im)
                    y_wide[at, pl.ds(m * rows + t, 1), :] = jnp.sum(out[0] + out[1], axis=0, keepdims=True)
            return tuple(tuple(own) for own in states)

        lax.fori_loop(0, rows // step, body, load_states(into_ref, batches, lanes))

    each_block(share, on_lanes)
    narrow(y_wide, u_wide, skip_ref, y_ref)


def back_kernel(
    batches,
    keep_ref,
    u_ref,
    g_ref,
    into_ref,
    behind_ref,
    par_ref,
    skip_ref,
    d_ref,
    sums_ref,
    skip_sum_ref,
    u_wide,
    g_wide,
    d_wide,
    kept,
):
    tokens, share = u_ref.shape
    rows = tokens // batches
    widen(u_ref, u_wide)
    widen(g_ref, g_wide)

    def on_lanes(at, lanes):
        turn, res = (load_pairs(par_ref, 2 * i, lanes) for i in range(2))

        def ahead(block, states):
            states = [list(own) for own in states]
            for i in range(step):
                t = block * step + i
                for m in range(batches):
                    keep = keep_ref[m, t]
                    row = u_wide[at, pl.ds(m * rows + t, 1), :]
                    for h in range(2):
                        re, im = times(turn[h][0] * keep, turn[h][1] * keep, *states[m][h])
                        kept[t, m, h, 0], kept[t, m, h, 1] = re, im
                        states[m][h] = (re + row, im)
            return tuple(tuple(own) for own in states)

        lax.fori_loop(0, rows // step, ahead, load_states(into_ref, batches, lanes))
        start = load_states(behind_ref, batches, lanes)

        def behind(block, carry):
            states, sums = [list(own) for own in carry[0]], list(carry[1])
            for i in range(step):
                t = rows - 1 - (block * step + i)
                for m in range(batches):
                    keep = keep_ref[m, t]
                    row = g_wide[at, pl.ds(m * rows + t, 1), :]
                    out = []
                    for h in range(2):
                        re, im = states[m][h]
                        re = re + row
                        x_re, x_im = kept[t, m, h, 0], kept[t, m, h, 1]
                        lag_re, lag_im = times(re, im, x_re, x_im)
                        g_re, g_im, w_re, w_im = sums[h]
                        sums[h] = (g_re + row * x_re, g_im + row * x_im, w_re + lag_re, w_im + lag_im)
                        out.append(res[h][0] * re - res[h][1] * im)
                        states[m][h] = times(turn[h][0] * keep, turn[h][1] * keep, re, im)
                    d_wide[at, pl.ds(m * rows + t, 1), :] = jnp.sum(out[0] + out[1], axis=0, keepdims=True)
            return tuple(tuple(own) for own in states), tuple(sums)

        zero = jnp.zeros((half_modes, lane_block), f32)
        skip_sum = jnp.sum(u_wide[at] * g_wide[at], axis=0, keepdims=True)
        skip_sum_ref[:, lanes] = skip_sum
        _, sums = lax.fori_loop(0, rows // step, behind, (start, ((zero,) * 4,) * 2))
        for h in range(2):
            g_re, g_im, w_re, w_im = sums[h]
            lag_re, lag_im = times(*res[h], w_re, w_im)
            sums_ref[0, h, :, lanes] = zero - lag_re
            sums_ref[1, h, :, lanes] = zero - lag_im
            sums_ref[2, h, :, lanes] = g_re + skip_sum
            sums_ref[3, h, :, lanes] = zero - g_im

    each_block(share, on_lanes)
    narrow(d_wide, g_wide, skip_ref, d_ref)


def in_vmem():
    return pl.BlockSpec(memory_space=pltpu.VMEM)


def in_smem():
    return pl.BlockSpec(memory_space=pltpu.SMEM)


def scratch_rows(u):
    return pltpu.VMEM((u.shape[1] // lane_block, u.shape[0], lane_block), f32)


def edge_states(u, keep, params, reverse):
    batches = keep.shape[0]
    return pl.pallas_call(
        functools.partial(edge_kernel, batches, reverse),
        out_shape=jax.ShapeDtypeStruct((batches, 2) + params.shape[1:], f32),
        in_specs=[in_smem(), in_vmem(), in_vmem()],
        out_specs=in_vmem(),
        scratch_shapes=[scratch_rows(u)],
        compiler_params=pltpu.CompilerParams(vmem_limit_bytes=48 << 20),
    )(keep, u, params)


def long_conv(keep, u, into, params, skips):
    return pl.pallas_call(
        functools.partial(conv_kernel, keep.shape[0]),
        out_shape=jax.ShapeDtypeStruct(u.shape, bf16),
        in_specs=[in_smem()] + [in_vmem()] * 4,
        out_specs=in_vmem(),
        scratch_shapes=[scratch_rows(u)] * 2,
        compiler_params=pltpu.CompilerParams(vmem_limit_bytes=48 << 20),
    )(keep, u, into, params, skips)


def long_conv_back(keep, u, g, into, behind, params, skips):
    batches, rows = keep.shape
    return pl.pallas_call(
        functools.partial(back_kernel, batches),
        out_shape=(
            jax.ShapeDtypeStruct(u.shape, bf16),
            jax.ShapeDtypeStruct((4,) + params.shape[1:], f32),
            jax.ShapeDtypeStruct((1, u.shape[1]), f32),
        ),
        in_specs=[in_smem()] + [in_vmem()] * 6,
        out_specs=(in_vmem(),) * 3,
        scratch_shapes=[scratch_rows(u)] * 3 + [pltpu.VMEM((rows, batches, 2, 2, half_modes, lane_block), f32)],
        compiler_params=pltpu.CompilerParams(vmem_limit_bytes=48 << 20),
    )(keep, u, g, into, behind, params, skips)


def shifted(array, axis, by):
    size = lax.axis_size(axis)
    pairs = [(i, i + by) for i in range(size) if 0 <= i + by < size]
    return lax.ppermute(array, axis, pairs)


def places_of(doc_lens, total):
    tokens = jnp.arange(total, dtype=jnp.int32)
    starts = jnp.cumsum(doc_lens, dtype=jnp.int32) - doc_lens
    begins = jnp.max(jnp.where(starts[None, :] <= tokens[:, None], starts[None, :], 0), axis=1)
    return tokens - begins


def dot_rows(left, right):
    return lax.dot_general(left, right, (((1,), (1,)), ((), ())), preferred_element_type=f32)


def dot_tokens(left, right):
    return lax.dot_general(left, right, (((0,), (0,)), ((), ())), preferred_element_type=f32)


def dot(left, right):
    return jnp.dot(left, right, preferred_element_type=f32)


def along_line(array, pairs):
    return lax.ppermute(array, "fsdp", pairs)


outer_pairs = [(0, 1), (1, 0), (2, 3), (3, 2)]
inner_pairs = [(1, 2), (2, 1)]


def after(value, *others):
    return lax.optimization_barrier((value,) + others)[0]


def gather_first(share):
    return along_line(share, outer_pairs), along_line(share, inner_pairs)


def gather_second(first):
    next_one, inner_one = first
    return along_line(inner_one, outer_pairs), along_line(next_one, inner_pairs)


def gather_last(second):
    return along_line(second[1], outer_pairs)


def gathered(share, first, second, last):
    own = lax.axis_index("fsdp")
    by_offset = (share, first[0], second[0] + second[1], last + first[1])
    blocks = []
    for place in range(4):
        offset = own ^ place
        block = by_offset[3]
        for k in range(3):
            block = jnp.where(offset == k, by_offset[k], block)
        blocks.append(block)
    return lax.optimization_barrier(jnp.concatenate(blocks, axis=1))


def gather_share(share):
    first = gather_first(share)
    second = gather_second(first)
    return gathered(share, first, second, gather_last(second))


def part_of(partial_sums, offset):
    share = partial_sums.shape[1] // 4
    return lax.dynamic_slice_in_dim(partial_sums, (lax.axis_index("fsdp") ^ offset) * share, share, 1)


def scatter_first(partial_sums):
    return along_line(part_of(partial_sums, 3), outer_pairs), along_line(part_of(partial_sums, 2), outer_pairs)


def scatter_second(partial_sums, first):
    far, near = first
    return (
        along_line(part_of(partial_sums, 2) + far, inner_pairs),
        along_line(part_of(partial_sums, 3) + near, inner_pairs),
    )


def scatter_last(partial_sums, second):
    return along_line(part_of(partial_sums, 1) + second[0], outer_pairs)


def scattered(partial_sums, second, last):
    return part_of(partial_sums, 0).astype(f32) + last.astype(f32) + second[1].astype(f32)


def scatter_offloaded(partial_sums):
    return lax.psum_scatter(partial_sums, "fsdp", scatter_dimension=1, tiled=True).astype(f32)


def sum_line(array):
    array = array + along_line(array, outer_pairs)
    return array + along_line(array, [(i, i ^ 2) for i in range(4)])


def swap_seq(array, bit):
    return lax.ppermute(array, "seq", [(i, i ^ (1 << bit)) for i in range(lax.axis_size("seq"))])


def gather_weight(shard):
    return lax.all_gather(shard, "seq", axis=0, tiled=True)


def of_core(left, core):
    count = lax.axis_size("seq")
    rows = left.shape[1] // count
    parts = [lax.dynamic_slice_in_dim(left, (2 * chip + core) * rows, rows, 1) for chip in range(count // 2)]
    return lax.optimization_barrier(jnp.concatenate(parts, axis=1))


def core_give(left, right):
    core = lax.axis_index("seq") % 2
    return lax.optimization_barrier(dot_tokens(of_core(left, 1 - core), right).astype(bf16))


def core_sum(left, right, got):
    own = dot_tokens(of_core(left, lax.axis_index("seq") % 2), right)
    return with_layout_constraint((own + got.astype(f32)).astype(bf16), Layout(major_to_minor=(0, 1)))


def chip_sums_offloaded(summed):
    count = lax.axis_size("seq")
    groups = [list(range(core, count, 2)) for core in range(2)]
    return lax.psum_scatter(summed, "seq", scatter_dimension=0, axis_index_groups=groups, tiled=True)


def chip_sums(summed, *before_last):
    count = lax.axis_size("seq")
    rank = lax.axis_index("seq")
    rows, bits = 2 * summed.shape[0] // count, count.bit_length() - 1
    by_bits = summed.reshape((2,) * (bits - 1) + (rows, summed.shape[1]))

    def halve(array, rest, bit):
        dim, mine = rest.index(bit), (rank >> bit) & 1
        keep = lax.dynamic_index_in_dim(array, mine, dim, keepdims=False)
        give = lax.dynamic_index_in_dim(array, 1 - mine, dim, keepdims=False)
        got = swap_seq(give.astype(bf16), bit)
        return keep.astype(f32) + got.astype(f32), [other for other in rest if other != bit]

    chip_bits = list(range(1, bits))
    middle = len(chip_bits) // 2
    parts = []
    for half, order in enumerate((chip_bits, chip_bits[middle:] + chip_bits[:middle])):
        part = lax.slice_in_dim(by_bits, half * rows // 2, (half + 1) * rows // 2, axis=bits - 1)
        rest = chip_bits[::-1]
        for bit in order[:-1]:
            part, rest = halve(part, rest, bit)
        part, rest = halve(after(part.astype(bf16), *before_last), rest, order[-1])
        parts.append(with_layout_constraint(part, Layout(major_to_minor=(0, 1))))
    return parts


def passing_factors(whole, power, reverse):
    count = lax.axis_size("seq")
    rank = lax.axis_index("seq")
    if reverse:
        rank, whole = count - 1 - rank, whole[:, ::-1]
    devices = jnp.arange(count)

    def factor(exponent, within):
        kept = jnp.min(jnp.where(within, whole, 1.0), axis=1)[:, None, None, None]
        return jnp.stack([part * kept for part in power(exponent)])

    steps = []
    for bit in range(count.bit_length() - 1):
        size = 1 << bit
        group = rank // size
        later = (group % 2).astype(f32)
        ahead = factor((rank % size).astype(f32), (devices // size == group) & (devices < rank)) * later
        last = factor(float(size), devices // size == (group | 1))
        steps.append((ahead, last))
    return lax.optimization_barrier(steps)


def through(edge, factors, reverse):
    count = lax.axis_size("seq")
    rank = lax.axis_index("seq")
    if reverse:
        rank = count - 1 - rank

    def grown(factor, state):
        re, im = times(factor[0], factor[1], state[:, 0], state[:, 1])
        return jnp.stack([re, im], axis=1)

    into = jnp.zeros_like(edge)
    for bit, (ahead, last) in enumerate(factors):
        later = (rank >> bit) & 1 == 1
        got = swap_seq(edge, bit)
        into = into + grown(ahead, got)
        if bit + 1 < len(factors):
            edge = jnp.where(later, edge, got) + grown(last, jnp.where(later, got, edge))
    return into


def sum_seq(array):
    for bit in range(lax.axis_size("seq").bit_length() - 1):
        array = array + swap_seq(array, bit)
    return array


def on_device(
    hidden_in,
    out_cot,
    doc_lengths,
    mixer_gain,
    in_proj,
    short_filter,
    decay_rate,
    mode_angle,
    residue_re,
    residue_im,
    skip_gain,
    out_proj,
    feed_gain,
    gate_proj,
    up_proj,
    down_proj,
):
    batches, rows, share = hidden_in.shape
    tokens = batches * rows
    width = mixer_gain.shape[0]
    seq_count = lax.axis_size("seq")
    seq_rank = lax.axis_index("seq")
    fsdp_rank = lax.axis_index("fsdp")
    total = rows * seq_count
    d_rows = in_proj.shape[0]

    x_share = hidden_in.reshape(tokens, share)
    cot_share = out_cot.reshape(tokens, share)
    x_rows = gather_share(x_share)
    x_all = x_rows.astype(f32)
    units = gate_proj.shape[1]
    w_in = gather_weight(jnp.concatenate([in_proj[:, j] for j in range(3)], axis=1))
    w_both = gather_weight(jnp.concatenate([out_proj.T, down_proj.T], axis=1))
    w_out, w_down = w_both[:, :share], w_both[:, share:]
    w_feed = gather_weight(jnp.concatenate([gate_proj, up_proj], axis=1))

    places = jnp.stack([places_of(doc_lengths[m], total) for m in range(batches)])
    keep = (places > 0).astype(f32)
    places_here = lax.dynamic_slice_in_dim(places, seq_rank * rows, rows, 1)
    masks = [(places_here >= lag).astype(f32)[:, :, None] for lag in range(3)]
    taps = short_filter.reshape(3, 3 * share)

    keep_here = lax.dynamic_slice_in_dim(keep, seq_rank * rows, rows, 1)
    whole = jnp.min(keep.reshape(batches, seq_count, rows), axis=2)
    rates, angles, res_re, res_im = (
        part.T.reshape(2, half_modes, share) for part in (decay_rate, mode_angle, residue_re, residue_im)
    )

    def power(devices):
        fading = jnp.exp(-(devices * rows) * rates)
        return fading * jnp.cos((devices * rows) * angles), fading * jnp.sin((devices * rows) * angles)

    fading = jnp.exp(-rates)
    modes = jnp.stack([fading * jnp.cos(angles), fading * jnp.sin(angles), res_re, res_im])
    skips = skip_gain[None]
    masked_taps = lax.optimization_barrier([taps[lag] * masks[lag] for lag in range(3)])
    factors = passing_factors(whole, power, False)
    back_factors = passing_factors(whole, power, True)

    scale_one = lax.rsqrt(jnp.mean(x_all * x_all, axis=-1, keepdims=True) + norm_eps)
    unit_one = x_all * scale_one
    normed_one = after((unit_one * mixer_gain).astype(bf16), modes, masked_taps, factors, back_factors)
    project = dot(normed_one, w_in).reshape(batches, rows, 3 * share)
    extended = jnp.concatenate([shifted(project[:, -2:], "seq", 1), project], axis=1)
    lagged = [extended[:, 2 - lag : 2 - lag + rows] for lag in range(3)]
    conv = sum(masked_taps[lag] * lagged[lag] for lag in range(3)).reshape(tokens, 3 * share)
    gate_one, gate_two, values = (conv[:, j * share : (j + 1) * share] for j in range(3))
    product = (gate_two * values).astype(bf16)
    cot_late = after(cot_share, product)
    cot_first = gather_first(cot_late)
    into = through(edge_states(product, keep_here, modes, False), factors, False)
    cot_second = gather_second(cot_first)
    mixed = long_conv(keep_here, product, after(into, *cot_first), modes, skips)
    cot_last = gather_last(cot_second)
    mixed = after(mixed, *cot_second).astype(f32)
    gated = (gate_one * mixed).astype(bf16)
    mix_part = dot_rows(gated, w_out).astype(bf16)
    mix_first = scatter_first(mix_part)
    mix_second = scatter_second(mix_part, mix_first)
    cot_all = gathered(cot_share, cot_first, cot_second, after(cot_last, mix_first[0]))
    d_hidden = lax.optimization_barrier(dot(cot_all, w_down))
    mix_last = scatter_last(mix_part, mix_second)
    stream = x_share.astype(f32) + scattered(mix_part, mix_second, mix_last)
    stream_all = gather_share(stream.astype(bf16)).astype(f32)
    scale_two = lax.rsqrt(jnp.mean(stream_all * stream_all, axis=-1, keepdims=True) + norm_eps)
    unit_two = stream_all * scale_two
    normed_two = lax.optimization_barrier((unit_two * feed_gain).astype(bf16))
    feed_pre = dot(normed_two, w_feed)
    gate_pre, up_pre = feed_pre[:, :units], feed_pre[:, units:]
    sigmoid = jax.nn.sigmoid(gate_pre)
    activated = gate_pre * sigmoid
    hidden = (activated * up_pre).astype(bf16)

    d_gate = d_hidden * up_pre * sigmoid * (1.0 + gate_pre * (1.0 - sigmoid))
    d_up = d_hidden * activated
    d_feed = jnp.concatenate([d_gate.astype(bf16), d_up.astype(bf16)], axis=1)
    along_two = jnp.sum(d_gate * gate_pre + d_up * up_pre, axis=-1)
    along_two = sum_line(along_two.reshape(-1, 128))
    part_two = dot_rows(d_feed, w_feed).astype(bf16)
    along_two = along_two.reshape(tokens, 1)
    dn_two = lax.psum_scatter(part_two, "fsdp", scatter_dimension=1, tiled=True)
    feed_got = swap_seq(core_give(normed_two, after(d_feed, part_two)), 0)
    down_got = swap_seq(core_give(cot_all, after(hidden, part_two)), 0)
    feed_sum = core_sum(normed_two, d_feed, feed_got)
    down_sum = core_sum(cot_all, hidden, down_got)

    def own_features(part):
        return lax.dynamic_slice_in_dim(part, fsdp_rank * share, share, 0)

    d_stream = (
        cot_share.astype(f32)
        + scale_two * own_features(feed_gain) * dn_two.astype(f32)
        - stream * (scale_two * scale_two * along_two / width)
    )
    d_share = d_stream.astype(bf16)
    d_mix = lax.all_gather(d_share, "fsdp", axis=1, tiled=True)
    down_part = dot_rows(after(hidden, d_share), w_down).astype(bf16)
    feed_sums = lax.optimization_barrier(jnp.concatenate([feed_sum, down_sum], axis=1))
    d_mix = after(d_mix, feed_sums, down_part)
    feed_own = chip_sums_offloaded(after(feed_sums, d_mix))

    d_gated = lax.optimization_barrier(dot(d_mix, w_out))
    down_first = scatter_first(after(down_part, d_gated))
    d_gate_one = d_gated * mixed
    d_mixed = (d_gated * gate_one).astype(bf16)
    behind = through(edge_states(d_mixed, keep_here, modes, True), back_factors, True)
    down_second = scatter_second(down_part, down_first)
    d_mix_late = after(d_mix, d_mixed)
    out_sum = core_sum(d_mix_late, gated, swap_seq(core_give(d_mix_late, gated), 0))
    down_last = scatter_last(down_part, down_second)
    feed_gain_part = jnp.sum(unit_two * after(part_two, d_mixed).astype(f32), axis=0)
    d_product, mode_sums, skip_sums = long_conv_back(
        keep_here, product, d_mixed, into, after(behind, *down_first), modes, skips
    )
    d_product = after(d_product, out_sum, feed_gain_part, *down_second)
    block_out = stream + scattered(down_part, down_second, down_last)
    d_product = d_product.astype(f32)
    d_conv = jnp.concatenate([d_gate_one, d_product * values, d_product * gate_two], axis=1)
    d_conv = d_conv.reshape(batches, rows, 3 * share)
    spread = sum(
        jnp.pad(taps[lag] * masks[lag] * d_conv, ((0, 0), (2 - lag, lag), (0, 0))) for lag in range(3)
    )
    returned = shifted(spread[:, :2], "seq", -1)
    d_project = spread[:, 2:] + jnp.pad(returned, ((0, 0), (rows - 2, 0), (0, 0)))
    d_project = d_project.astype(bf16).reshape(tokens, 3 * share)
    part_one = dot_rows(d_project, w_in).astype(bf16)
    dn_one = lax.psum_scatter(after(part_one, feed_own), "fsdp", scatter_dimension=1, tiled=True)
    in_give = core_give(normed_one, after(d_project, part_one, feed_own))
    in_got = swap_seq(in_give, 0)
    d_conv, late_project, late_part = lax.optimization_barrier((d_conv, d_project, part_one, in_give))[:3]
    short_part = jnp.stack([jnp.sum(masks[lag] * lagged[lag] * d_conv, axis=(0, 1)) for lag in range(3)])
    mixer_gain_part = jnp.sum(unit_one * late_part.astype(f32), axis=0)
    in_sum = core_sum(normed_one, d_project, after(in_got, mixer_gain_part))
    small = after((mixer_gain_part, feed_gain_part, short_part, mode_sums, skip_sums), in_sum)
    small = jnp.concatenate([part.reshape(-1, share) for part in small])
    for bit in range(1, seq_count.bit_length() - 1):
        small = small + swap_seq(small, bit)
    in_out = jnp.concatenate([in_sum, out_sum], axis=1)
    feed_own = after(feed_own, in_sum)
    gate_grad, up_grad, down_grad = (
        feed_own[:, i * units : (i + 1) * units].astype(f32) for i in range(3)
    )
    in_out = chip_sums(after(in_out, small), dn_one)
    small = small + swap_seq(small, 0)
    gain_rows = 2 * width // share
    along_one = jnp.sum(late_project.astype(f32) * project.reshape(tokens, 3 * share), axis=-1)
    lined = sum_line(jnp.concatenate([small[:gain_rows], along_one.reshape(-1, share)]))
    gains, along_one = lined[:gain_rows].reshape(2, width), lined[gain_rows:].reshape(tokens, 1)
    d_x = (
        d_stream
        + scale_one * own_features(mixer_gain) * dn_one.astype(f32)
        - x_share.astype(f32) * (scale_one * scale_one * along_one / width)
    )

    branches = [jnp.concatenate([half[:, j * share : (j + 1) * share] for half in in_out]) for j in range(4)]
    in_grad, out_grad = jnp.stack(branches[:3]).transpose(1, 0, 2), branches[3]
    short_grad = small[gain_rows : gain_rows + 9].reshape(3, 3, share)
    filters = small[gain_rows + 9 :]
    by_chan = filters[:-1].reshape(4, 2 * half_modes, share).transpose(0, 2, 1)
    return (
        block_out.astype(bf16).reshape(hidden_in.shape),
        d_x.reshape(hidden_in.shape),
        gains[0],
        in_grad,
        short_grad,
        by_chan[0],
        by_chan[1],
        by_chan[2],
        by_chan[3],
        filters[-1],
        out_grad.T,
        gains[1],
        gate_grad,
        up_grad,
        down_grad.T,
    )


def solution(mesh):
    tokens = P(None, "seq", "fsdp")
    chan_rows = P("fsdp", None)
    d_rows = P("seq", "fsdp")
    d_cols = P("fsdp", "seq")
    in_specs = (
        tokens,
        tokens,
        P(),
        P(),
        P("seq", None, "fsdp"),
        P(None, None, "fsdp"),
        chan_rows,
        chan_rows,
        chan_rows,
        chan_rows,
        P("fsdp"),
        d_cols,
        P(),
        d_rows,
        d_rows,
        d_cols,
    )
    out_specs = (
        tokens,
        tokens,
        P(),
        P("seq", None, "fsdp"),
        P(None, None, "fsdp"),
        chan_rows,
        chan_rows,
        chan_rows,
        chan_rows,
        P("fsdp"),
        d_cols,
        P(),
        d_rows,
        d_rows,
        d_cols,
    )
    return jax.shard_map(on_device, mesh=mesh, in_specs=in_specs, out_specs=out_specs, check_vma=False)
```

```python
import functools

import jax
import jax.numpy as jnp
from jax import lax
from jax.experimental import pallas as pl
from jax.experimental.pallas import tpu as pltpu
from jax.experimental.layout import Layout, with_layout_constraint
from jax.sharding import PartitionSpec as P

norm_eps = 1e-05
half_modes = 8
f32 = jnp.float32
bf16 = jnp.bfloat16


lane_block = 128
step = 16


def times(a_re, a_im, b_re, b_im):
    return a_re * b_re - a_im * b_im, a_re * b_im + a_im * b_re


def each_block(width, body):
    def run(block, carry):
        body(block, pl.ds(pl.multiple_of(block * lane_block, lane_block), lane_block))
        return carry

    lax.fori_loop(0, width // lane_block, run, 0)


def widen(src_ref, dst_ref):
    for block in range(dst_ref.shape[0]):
        dst_ref[block] = src_ref[:, block * lane_block : (block + 1) * lane_block].astype(f32)


def narrow(src_ref, direct_ref, skip_ref, dst_ref):
    for block in range(src_ref.shape[0]):
        lanes = slice(block * lane_block, (block + 1) * lane_block)
        dst_ref[:, lanes] = (src_ref[block] + skip_ref[:, lanes] * direct_ref[block]).astype(bf16)


def load_pairs(ref, index, lanes):
    return [(ref[index, h, :, lanes], ref[index + 1, h, :, lanes]) for h in range(2)]


def edge_kernel(batches, reverse, keep_ref, u_ref, par_ref, edge_ref, u_wide):
    tokens, share = u_ref.shape
    rows = tokens // batches
    widen(u_ref, u_wide)

    def on_lanes(at, lanes):
        turn = load_pairs(par_ref, 0, lanes)

        def body(block, states):
            states = [list(own) for own in states]
            for i in range(step):
                t = block * step + i
                t = rows - 1 - t if reverse else t
                for m in range(batches):
                    keep = keep_ref[m, t]
                    row = u_wide[at, pl.ds(m * rows + t, 1), :]
                    for h in range(2):
                        re, im = states[m][h]
                        turn_re, turn_im = turn[h][0] * keep, turn[h][1] * keep
                        if reverse:
                            states[m][h] = times(turn_re, turn_im, re + row, im)
                        else:
                            re, im = times(turn_re, turn_im, re, im)
                            states[m][h] = (re + row, im)
            return tuple(tuple(own) for own in states)

        zero = jnp.zeros((half_modes, lane_block), f32)
        states = lax.fori_loop(0, rows // step, body, (((zero, zero),) * 2,) * batches)
        for m in range(batches):
            for h in range(2):
                edge_ref[m, 0, h, :, lanes], edge_ref[m, 1, h, :, lanes] = states[m][h]

    each_block(share, on_lanes)


def load_states(ref, batches, lanes):
    return tuple(
        tuple((ref[m, 0, h, :, lanes], ref[m, 1, h, :, lanes]) for h in range(2)) for m in range(batches)
    )


def conv_kernel(batches, keep_ref, u_ref, into_ref, par_ref, skip_ref, y_ref, u_wide, y_wide):
    tokens, share = u_ref.shape
    rows = tokens // batches
    widen(u_ref, u_wide)

    def on_lanes(at, lanes):
        turn, res = (load_pairs(par_ref, 2 * i, lanes) for i in range(2))

        def body(block, states):
            states = [list(own) for own in states]
            for i in range(step):
                t = block * step + i
                for m in range(batches):
                    keep = keep_ref[m, t]
                    row = u_wide[at, pl.ds(m * rows + t, 1), :]
                    out = []
                    for h in range(2):
                        re, im = times(turn[h][0] * keep, turn[h][1] * keep, *states[m][h])
                        re = re + row
                        states[m][h] = (re, im)
                        out.append(res[h][0] * re - res[h][1] * im)
                    y_wide[at, pl.ds(m * rows + t, 1), :] = jnp.sum(out[0] + out[1], axis=0, keepdims=True)
            return tuple(tuple(own) for own in states)

        lax.fori_loop(0, rows // step, body, load_states(into_ref, batches, lanes))

    each_block(share, on_lanes)
    narrow(y_wide, u_wide, skip_ref, y_ref)


def back_kernel(
    batches,
    keep_ref,
    u_ref,
    g_ref,
    into_ref,
    behind_ref,
    par_ref,
    skip_ref,
    d_ref,
    sums_ref,
    skip_sum_ref,
    u_wide,
    g_wide,
    d_wide,
    kept,
):
    tokens, share = u_ref.shape
    rows = tokens // batches
    widen(u_ref, u_wide)
    widen(g_ref, g_wide)

    def on_lanes(at, lanes):
        turn, res = (load_pairs(par_ref, 2 * i, lanes) for i in range(2))

        def ahead(block, states):
            states = [list(own) for own in states]
            for i in range(step):
                t = block * step + i
                for m in range(batches):
                    keep = keep_ref[m, t]
                    row = u_wide[at, pl.ds(m * rows + t, 1), :]
                    for h in range(2):
                        re, im = times(turn[h][0] * keep, turn[h][1] * keep, *states[m][h])
                        kept[t, m, h, 0], kept[t, m, h, 1] = re, im
                        states[m][h] = (re + row, im)
            return tuple(tuple(own) for own in states)

        lax.fori_loop(0, rows // step, ahead, load_states(into_ref, batches, lanes))
        start = load_states(behind_ref, batches, lanes)

        def behind(block, carry):
            states, sums = [list(own) for own in carry[0]], list(carry[1])
            for i in range(step):
                t = rows - 1 - (block * step + i)
                for m in range(batches):
                    keep = keep_ref[m, t]
                    row = g_wide[at, pl.ds(m * rows + t, 1), :]
                    out = []
                    for h in range(2):
                        re, im = states[m][h]
                        re = re + row
                        x_re, x_im = kept[t, m, h, 0], kept[t, m, h, 1]
                        lag_re, lag_im = times(re, im, x_re, x_im)
                        g_re, g_im, w_re, w_im = sums[h]
                        sums[h] = (g_re + row * x_re, g_im + row * x_im, w_re + lag_re, w_im + lag_im)
                        out.append(res[h][0] * re - res[h][1] * im)
                        states[m][h] = times(turn[h][0] * keep, turn[h][1] * keep, re, im)
                    d_wide[at, pl.ds(m * rows + t, 1), :] = jnp.sum(out[0] + out[1], axis=0, keepdims=True)
            return tuple(tuple(own) for own in states), tuple(sums)

        zero = jnp.zeros((half_modes, lane_block), f32)
        skip_sum = jnp.sum(u_wide[at] * g_wide[at], axis=0, keepdims=True)
        skip_sum_ref[:, lanes] = skip_sum
        _, sums = lax.fori_loop(0, rows // step, behind, (start, ((zero,) * 4,) * 2))
        for h in range(2):
            g_re, g_im, w_re, w_im = sums[h]
            lag_re, lag_im = times(*res[h], w_re, w_im)
            sums_ref[0, h, :, lanes] = zero - lag_re
            sums_ref[1, h, :, lanes] = zero - lag_im
            sums_ref[2, h, :, lanes] = g_re + skip_sum
            sums_ref[3, h, :, lanes] = zero - g_im

    each_block(share, on_lanes)
    narrow(d_wide, g_wide, skip_ref, d_ref)


def in_vmem():
    return pl.BlockSpec(memory_space=pltpu.VMEM)


def in_smem():
    return pl.BlockSpec(memory_space=pltpu.SMEM)


def scratch_rows(u):
    return pltpu.VMEM((u.shape[1] // lane_block, u.shape[0], lane_block), f32)


def edge_states(u, keep, params, reverse):
    batches = keep.shape[0]
    return pl.pallas_call(
        functools.partial(edge_kernel, batches, reverse),
        out_shape=jax.ShapeDtypeStruct((batches, 2) + params.shape[1:], f32),
        in_specs=[in_smem(), in_vmem(), in_vmem()],
        out_specs=in_vmem(),
        scratch_shapes=[scratch_rows(u)],
        compiler_params=pltpu.CompilerParams(vmem_limit_bytes=48 << 20),
    )(keep, u, params)


def long_conv(keep, u, into, params, skips):
    return pl.pallas_call(
        functools.partial(conv_kernel, keep.shape[0]),
        out_shape=jax.ShapeDtypeStruct(u.shape, bf16),
        in_specs=[in_smem()] + [in_vmem()] * 4,
        out_specs=in_vmem(),
        scratch_shapes=[scratch_rows(u)] * 2,
        compiler_params=pltpu.CompilerParams(vmem_limit_bytes=48 << 20),
    )(keep, u, into, params, skips)


def long_conv_back(keep, u, g, into, behind, params, skips):
    batches, rows = keep.shape
    return pl.pallas_call(
        functools.partial(back_kernel, batches),
        out_shape=(
            jax.ShapeDtypeStruct(u.shape, bf16),
            jax.ShapeDtypeStruct((4,) + params.shape[1:], f32),
            jax.ShapeDtypeStruct((1, u.shape[1]), f32),
        ),
        in_specs=[in_smem()] + [in_vmem()] * 6,
        out_specs=(in_vmem(),) * 3,
        scratch_shapes=[scratch_rows(u)] * 3 + [pltpu.VMEM((rows, batches, 2, 2, half_modes, lane_block), f32)],
        compiler_params=pltpu.CompilerParams(vmem_limit_bytes=48 << 20),
    )(keep, u, g, into, behind, params, skips)


def shifted(array, axis, by):
    size = lax.axis_size(axis)
    pairs = [(i, i + by) for i in range(size) if 0 <= i + by < size]
    return lax.ppermute(array, axis, pairs)


def places_of(doc_lens, total):
    tokens = jnp.arange(total, dtype=jnp.int32)
    starts = jnp.cumsum(doc_lens, dtype=jnp.int32) - doc_lens
    begins = jnp.max(jnp.where(starts[None, :] <= tokens[:, None], starts[None, :], 0), axis=1)
    return tokens - begins


def dot_rows(left, right):
    return lax.dot_general(left, right, (((1,), (1,)), ((), ())), preferred_element_type=f32)


def dot_tokens(left, right):
    return lax.dot_general(left, right, (((0,), (0,)), ((), ())), preferred_element_type=f32)


def dot(left, right):
    return jnp.dot(left, right, preferred_element_type=f32)


def along_line(array, pairs):
    return lax.ppermute(array, "fsdp", pairs)


outer_pairs = [(0, 1), (1, 0), (2, 3), (3, 2)]
inner_pairs = [(1, 2), (2, 1)]


def after(value, *others):
    return lax.optimization_barrier((value,) + others)[0]


def gather_first(share):
    return along_line(share, outer_pairs), along_line(share, inner_pairs)


def gather_second(first):
    next_one, inner_one = first
    return along_line(inner_one, outer_pairs), along_line(next_one, inner_pairs)


def gather_last(second):
    return along_line(second[1], outer_pairs)


def gathered(share, first, second, last):
    own = lax.axis_index("fsdp")
    by_offset = (share, first[0], second[0] + second[1], last + first[1])
    blocks = []
    for place in range(4):
        offset = own ^ place
        block = by_offset[3]
        for k in range(3):
            block = jnp.where(offset == k, by_offset[k], block)
        blocks.append(block)
    return lax.optimization_barrier(jnp.concatenate(blocks, axis=1))


def gather_share(share):
    first = gather_first(share)
    second = gather_second(first)
    return gathered(share, first, second, gather_last(second))


def part_of(partial_sums, offset):
    share = partial_sums.shape[1] // 4
    return lax.dynamic_slice_in_dim(partial_sums, (lax.axis_index("fsdp") ^ offset) * share, share, 1)


def scatter_first(partial_sums):
    return along_line(part_of(partial_sums, 3), outer_pairs), along_line(part_of(partial_sums, 2), outer_pairs)


def scatter_second(partial_sums, first):
    far, near = first
    return (
        along_line(part_of(partial_sums, 2) + far, inner_pairs),
        along_line(part_of(partial_sums, 3) + near, inner_pairs),
    )


def scatter_last(partial_sums, second):
    return along_line(part_of(partial_sums, 1) + second[0], outer_pairs)


def scattered(partial_sums, second, last):
    return part_of(partial_sums, 0).astype(f32) + last.astype(f32) + second[1].astype(f32)


def scatter_offloaded(partial_sums):
    return lax.psum_scatter(partial_sums, "fsdp", scatter_dimension=1, tiled=True).astype(f32)


def sum_line(array):
    array = array + along_line(array, outer_pairs)
    return array + along_line(array, [(i, i ^ 2) for i in range(4)])


def swap_seq(array, bit):
    return lax.ppermute(array, "seq", [(i, i ^ (1 << bit)) for i in range(lax.axis_size("seq"))])


def gather_weight(shard):
    return lax.all_gather(shard, "seq", axis=0, tiled=True)


def of_core(left, core):
    count = lax.axis_size("seq")
    rows = left.shape[1] // count
    parts = [lax.dynamic_slice_in_dim(left, (2 * chip + core) * rows, rows, 1) for chip in range(count // 2)]
    return lax.optimization_barrier(jnp.concatenate(parts, axis=1))


def core_give(left, right):
    core = lax.axis_index("seq") % 2
    return lax.optimization_barrier(dot_tokens(of_core(left, 1 - core), right).astype(bf16))


def core_sum(left, right, got):
    own = dot_tokens(of_core(left, lax.axis_index("seq") % 2), right)
    return with_layout_constraint((own + got.astype(f32)).astype(bf16), Layout(major_to_minor=(0, 1)))


def chip_sums_offloaded(summed):
    count = lax.axis_size("seq")
    groups = [list(range(core, count, 2)) for core in range(2)]
    return lax.psum_scatter(summed, "seq", scatter_dimension=0, axis_index_groups=groups, tiled=True)


def chip_sums(summed, *before_last):
    count = lax.axis_size("seq")
    rank = lax.axis_index("seq")
    rows, bits = 2 * summed.shape[0] // count, count.bit_length() - 1
    by_bits = summed.reshape((2,) * (bits - 1) + (rows, summed.shape[1]))

    def halve(array, rest, bit):
        dim, mine = rest.index(bit), (rank >> bit) & 1
        keep = lax.dynamic_index_in_dim(array, mine, dim, keepdims=False)
        give = lax.dynamic_index_in_dim(array, 1 - mine, dim, keepdims=False)
        got = swap_seq(give.astype(bf16), bit)
        return keep.astype(f32) + got.astype(f32), [other for other in rest if other != bit]

    chip_bits = list(range(1, bits))
    middle = len(chip_bits) // 2
    parts = []
    for half, order in enumerate((chip_bits, chip_bits[middle:] + chip_bits[:middle])):
        part = lax.slice_in_dim(by_bits, half * rows // 2, (half + 1) * rows // 2, axis=bits - 1)
        rest = chip_bits[::-1]
        for bit in order[:-1]:
            part, rest = halve(part, rest, bit)
        part, rest = halve(after(part.astype(bf16), *before_last) if before_last else part, rest, order[-1])
        parts.append(with_layout_constraint(part, Layout(major_to_minor=(0, 1))))
    return parts


def passing_factors(whole, power, reverse):
    count = lax.axis_size("seq")
    rank = lax.axis_index("seq")
    if reverse:
        rank, whole = count - 1 - rank, whole[:, ::-1]
    devices = jnp.arange(count)

    def factor(exponent, within):
        kept = jnp.min(jnp.where(within, whole, 1.0), axis=1)[:, None, None, None]
        return jnp.stack([part * kept for part in power(exponent)])

    steps = []
    for bit in range(count.bit_length() - 1):
        size = 1 << bit
        group = rank // size
        later = (group % 2).astype(f32)
        ahead = factor((rank % size).astype(f32), (devices // size == group) & (devices < rank)) * later
        last = factor(float(size), devices // size == (group | 1))
        steps.append((ahead, last))
    return lax.optimization_barrier(steps)


def through(edge, factors, reverse):
    count = lax.axis_size("seq")
    rank = lax.axis_index("seq")
    if reverse:
        rank = count - 1 - rank

    def grown(factor, state):
        re, im = times(factor[0], factor[1], state[:, 0], state[:, 1])
        return jnp.stack([re, im], axis=1)

    into = jnp.zeros_like(edge)
    for bit, (ahead, last) in enumerate(factors):
        later = (rank >> bit) & 1 == 1
        got = swap_seq(edge, bit)
        into = into + grown(ahead, got)
        if bit + 1 < len(factors):
            edge = jnp.where(later, edge, got) + grown(last, jnp.where(later, got, edge))
    return into


def sum_seq(array):
    for bit in range(lax.axis_size("seq").bit_length() - 1):
        array = array + swap_seq(array, bit)
    return array


def on_device(
    hidden_in,
    out_cot,
    doc_lengths,
    mixer_gain,
    in_proj,
    short_filter,
    decay_rate,
    mode_angle,
    residue_re,
    residue_im,
    skip_gain,
    out_proj,
    feed_gain,
    gate_proj,
    up_proj,
    down_proj,
):
    batches, rows, share = hidden_in.shape
    tokens = batches * rows
    width = mixer_gain.shape[0]
    seq_count = lax.axis_size("seq")
    seq_rank = lax.axis_index("seq")
    fsdp_rank = lax.axis_index("fsdp")
    total = rows * seq_count
    d_rows = in_proj.shape[0]

    x_share = hidden_in.reshape(tokens, share)
    cot_share = out_cot.reshape(tokens, share)
    x_rows = gather_share(x_share)
    x_all = x_rows.astype(f32)
    units = gate_proj.shape[1]
    w_in = gather_weight(jnp.concatenate([in_proj[:, j] for j in range(3)], axis=1))
    w_both = gather_weight(jnp.concatenate([out_proj.T, down_proj.T], axis=1))
    w_out, w_down = w_both[:, :share], w_both[:, share:]
    w_feed = gather_weight(jnp.concatenate([gate_proj, up_proj], axis=1))

    places = jnp.stack([places_of(doc_lengths[m], total) for m in range(batches)])
    keep = (places > 0).astype(f32)
    places_here = lax.dynamic_slice_in_dim(places, seq_rank * rows, rows, 1)
    masks = [(places_here >= lag).astype(f32)[:, :, None] for lag in range(3)]
    taps = short_filter.reshape(3, 3 * share)

    keep_here = lax.dynamic_slice_in_dim(keep, seq_rank * rows, rows, 1)
    whole = jnp.min(keep.reshape(batches, seq_count, rows), axis=2)
    rates, angles, res_re, res_im = (
        part.T.reshape(2, half_modes, share) for part in (decay_rate, mode_angle, residue_re, residue_im)
    )

    def power(devices):
        fading = jnp.exp(-(devices * rows) * rates)
        return fading * jnp.cos((devices * rows) * angles), fading * jnp.sin((devices * rows) * angles)

    fading = jnp.exp(-rates)
    modes = jnp.stack([fading * jnp.cos(angles), fading * jnp.sin(angles), res_re, res_im])
    skips = skip_gain[None]
    masked_taps = lax.optimization_barrier([taps[lag] * masks[lag] for lag in range(3)])
    factors = passing_factors(whole, power, False)
    back_factors = passing_factors(whole, power, True)

    scale_one = lax.rsqrt(jnp.mean(x_all * x_all, axis=-1, keepdims=True) + norm_eps)
    unit_one = x_all * scale_one
    normed_one = after((unit_one * mixer_gain).astype(bf16), modes, masked_taps, factors, back_factors)
    project = dot(normed_one, w_in).reshape(batches, rows, 3 * share)
    extended = jnp.concatenate([shifted(project[:, -2:], "seq", 1), project], axis=1)
    lagged = [extended[:, 2 - lag : 2 - lag + rows] for lag in range(3)]
    conv = sum(masked_taps[lag] * lagged[lag] for lag in range(3)).reshape(tokens, 3 * share)
    gate_one, gate_two, values = (conv[:, j * share : (j + 1) * share] for j in range(3))
    product = (gate_two * values).astype(bf16)
    cot_late = after(cot_share, product)
    cot_first = gather_first(cot_late)
    into = through(edge_states(product, keep_here, modes, False), factors, False)
    cot_second = gather_second(cot_first)
    mixed = long_conv(keep_here, product, after(into, *cot_first), modes, skips)
    cot_last = gather_last(cot_second)
    mixed = after(mixed, *cot_second).astype(f32)
    gated = (gate_one * mixed).astype(bf16)
    mix_part = dot_rows(gated, w_out).astype(bf16)
    mix_first = scatter_first(mix_part)
    mix_second = scatter_second(mix_part, mix_first)
    cot_all = gathered(cot_share, cot_first, cot_second, after(cot_last, mix_first[0]))
    d_hidden = lax.optimization_barrier(dot(cot_all, w_down))
    mix_last = scatter_last(mix_part, mix_second)
    stream = x_share.astype(f32) + scattered(mix_part, mix_second, mix_last)
    stream_all = gather_share(stream.astype(bf16)).astype(f32)
    scale_two = lax.rsqrt(jnp.mean(stream_all * stream_all, axis=-1, keepdims=True) + norm_eps)
    unit_two = stream_all * scale_two
    normed_two = lax.optimization_barrier((unit_two * feed_gain).astype(bf16))
    feed_pre = dot(normed_two, w_feed)
    gate_pre, up_pre = feed_pre[:, :units], feed_pre[:, units:]
    sigmoid = jax.nn.sigmoid(gate_pre)
    activated = gate_pre * sigmoid
    hidden = (activated * up_pre).astype(bf16)

    d_gate = d_hidden * up_pre * sigmoid * (1.0 + gate_pre * (1.0 - sigmoid))
    d_up = d_hidden * activated
    d_feed = jnp.concatenate([d_gate.astype(bf16), d_up.astype(bf16)], axis=1)
    along_two = jnp.sum(d_gate * gate_pre + d_up * up_pre, axis=-1)
    along_two = sum_line(along_two.reshape(-1, 128))
    part_two = dot_rows(d_feed, w_feed).astype(bf16)
    along_two = along_two.reshape(tokens, 1)
    dn_two = lax.psum_scatter(part_two, "fsdp", scatter_dimension=1, tiled=True)
    feed_got = swap_seq(core_give(normed_two, after(d_feed, part_two)), 0)
    down_got = swap_seq(core_give(cot_all, after(hidden, part_two)), 0)
    feed_sum = core_sum(normed_two, d_feed, feed_got)
    down_sum = core_sum(cot_all, hidden, down_got)

    def own_features(part):
        return lax.dynamic_slice_in_dim(part, fsdp_rank * share, share, 0)

    d_stream = (
        cot_share.astype(f32)
        + scale_two * own_features(feed_gain) * dn_two.astype(f32)
        - stream * (scale_two * scale_two * along_two / width)
    )
    d_share = d_stream.astype(bf16)
    d_mix = lax.all_gather(d_share, "fsdp", axis=1, tiled=True)
    down_part = dot_rows(after(hidden, d_share), w_down).astype(bf16)
    feed_sums = lax.optimization_barrier(jnp.concatenate([feed_sum, down_sum], axis=1))
    d_mix = after(d_mix, feed_sums, down_part)
    feed_own = chip_sums_offloaded(after(feed_sums, d_mix))

    d_gated = lax.optimization_barrier(dot(d_mix, w_out))
    down_first = scatter_first(after(down_part, d_gated))
    d_gate_one = d_gated * mixed
    d_mixed = (d_gated * gate_one).astype(bf16)
    behind = through(edge_states(d_mixed, keep_here, modes, True), back_factors, True)
    down_second = scatter_second(down_part, down_first)
    d_mix_late = after(d_mix, d_mixed)
    out_sum = core_sum(d_mix_late, gated, swap_seq(core_give(d_mix_late, gated), 0))
    down_last = scatter_last(down_part, down_second)
    feed_gain_part = jnp.sum(unit_two * after(part_two, d_mixed).astype(f32), axis=0)
    d_product, mode_sums, skip_sums = long_conv_back(
        keep_here, product, d_mixed, into, after(behind, *down_first), modes, skips
    )
    d_product = after(d_product, out_sum, feed_gain_part, *down_second)
    block_out = stream + scattered(down_part, down_second, down_last)
    d_product = d_product.astype(f32)
    d_conv = jnp.concatenate([d_gate_one, d_product * values, d_product * gate_two], axis=1)
    d_conv = d_conv.reshape(batches, rows, 3 * share)
    spread = sum(
        jnp.pad(taps[lag] * masks[lag] * d_conv, ((0, 0), (2 - lag, lag), (0, 0))) for lag in range(3)
    )
    returned = shifted(spread[:, :2], "seq", -1)
    d_project = spread[:, 2:] + jnp.pad(returned, ((0, 0), (rows - 2, 0), (0, 0)))
    d_project = d_project.astype(bf16).reshape(tokens, 3 * share)
    part_one = dot_rows(d_project, w_in).astype(bf16)
    dn_one = lax.psum_scatter(after(part_one, feed_own), "fsdp", scatter_dimension=1, tiled=True)
    in_give = core_give(normed_one, after(d_project, part_one))
    in_got = swap_seq(in_give, 0)
    in_sum = core_sum(normed_one, d_project, in_got)
    in_out = chip_sums(jnp.concatenate([in_sum, out_sum], axis=1), dn_one)
    d_conv, late_project, late_part = lax.optimization_barrier((d_conv, d_project, part_one, in_sum, feed_own))[:3]
    short_part = jnp.stack([jnp.sum(masks[lag] * lagged[lag] * d_conv, axis=(0, 1)) for lag in range(3)])
    mixer_gain_part = jnp.sum(unit_one * late_part.astype(f32), axis=0)
    small = [mixer_gain_part, feed_gain_part, short_part, mode_sums, skip_sums]
    small = jnp.concatenate([part.reshape(-1, share) for part in small])
    for bit in range(1, seq_count.bit_length() - 1):
        small = small + swap_seq(small, bit)
    feed_own = after(feed_own, in_sum)
    gate_grad, up_grad, down_grad = (
        feed_own[:, i * units : (i + 1) * units].astype(f32) for i in range(3)
    )
    small = small
    small = small + swap_seq(small, 0)
    gain_rows = 2 * width // share
    along_one = jnp.sum(late_project.astype(f32) * project.reshape(tokens, 3 * share), axis=-1)
    lined = sum_line(jnp.concatenate([small[:gain_rows], along_one.reshape(-1, share)]))
    gains, along_one = lined[:gain_rows].reshape(2, width), lined[gain_rows:].reshape(tokens, 1)
    d_x = (
        d_stream
        + scale_one * own_features(mixer_gain) * dn_one.astype(f32)
        - x_share.astype(f32) * (scale_one * scale_one * along_one / width)
    )

    branches = [jnp.concatenate([half[:, j * share : (j + 1) * share] for half in in_out]) for j in range(4)]
    in_grad, out_grad = jnp.stack(branches[:3]).transpose(1, 0, 2), branches[3]
    short_grad = small[gain_rows : gain_rows + 9].reshape(3, 3, share)
    filters = small[gain_rows + 9 :]
    by_chan = filters[:-1].reshape(4, 2 * half_modes, share).transpose(0, 2, 1)
    return (
        block_out.astype(bf16).reshape(hidden_in.shape),
        d_x.reshape(hidden_in.shape),
        gains[0],
        in_grad,
        short_grad,
        by_chan[0],
        by_chan[1],
        by_chan[2],
        by_chan[3],
        filters[-1],
        out_grad.T,
        gains[1],
        gate_grad,
        up_grad,
        down_grad.T,
    )


def solution(mesh):
    tokens = P(None, "seq", "fsdp")
    chan_rows = P("fsdp", None)
    d_rows = P("seq", "fsdp")
    d_cols = P("fsdp", "seq")
    in_specs = (
        tokens,
        tokens,
        P(),
        P(),
        P("seq", None, "fsdp"),
        P(None, None, "fsdp"),
        chan_rows,
        chan_rows,
        chan_rows,
        chan_rows,
        P("fsdp"),
        d_cols,
        P(),
        d_rows,
        d_rows,
        d_cols,
    )
    out_specs = (
        tokens,
        tokens,
        P(),
        P("seq", None, "fsdp"),
        P(None, None, "fsdp"),
        chan_rows,
        chan_rows,
        chan_rows,
        chan_rows,
        P("fsdp"),
        d_cols,
        P(),
        d_rows,
        d_rows,
        d_cols,
    )
    return jax.shard_map(on_device, mesh=mesh, in_specs=in_specs, out_specs=out_specs, check_vma=False)
```

```python
import functools

import jax
import jax.numpy as jnp
from jax import lax
from jax.experimental import pallas as pl
from jax.experimental.pallas import tpu as pltpu
from jax.experimental.layout import Layout, with_layout_constraint
from jax.sharding import PartitionSpec as P

norm_eps = 1e-05
half_modes = 8
f32 = jnp.float32
bf16 = jnp.bfloat16


lane_block = 128
step = 32


def times(a_re, a_im, b_re, b_im):
    return a_re * b_re - a_im * b_im, a_re * b_im + a_im * b_re


def each_block(width, body):
    def run(block, carry):
        body(block, pl.ds(pl.multiple_of(block * lane_block, lane_block), lane_block))
        return carry

    lax.fori_loop(0, width // lane_block, run, 0)


def widen(src_ref, dst_ref):
    for block in range(dst_ref.shape[0]):
        dst_ref[block] = src_ref[:, block * lane_block : (block + 1) * lane_block].astype(f32)


def narrow(src_ref, direct_ref, skip_ref, dst_ref):
    for block in range(src_ref.shape[0]):
        lanes = slice(block * lane_block, (block + 1) * lane_block)
        dst_ref[:, lanes] = (src_ref[block] + skip_ref[:, lanes] * direct_ref[block]).astype(bf16)


def load_pairs(ref, index, lanes):
    return [(ref[index, h, :, lanes], ref[index + 1, h, :, lanes]) for h in range(2)]


def edge_kernel(batches, reverse, keep_ref, u_ref, par_ref, edge_ref, u_wide):
    tokens, share = u_ref.shape
    rows = tokens // batches
    widen(u_ref, u_wide)

    def on_lanes(at, lanes):
        turn = load_pairs(par_ref, 0, lanes)

        def body(block, states):
            states = [list(own) for own in states]
            for i in range(step):
                t = block * step + i
                t = rows - 1 - t if reverse else t
                for m in range(batches):
                    keep = keep_ref[m, t]
                    row = u_wide[at, pl.ds(m * rows + t, 1), :]
                    for h in range(2):
                        re, im = states[m][h]
                        turn_re, turn_im = turn[h][0] * keep, turn[h][1] * keep
                        if reverse:
                            states[m][h] = times(turn_re, turn_im, re + row, im)
                        else:
                            re, im = times(turn_re, turn_im, re, im)
                            states[m][h] = (re + row, im)
            return tuple(tuple(own) for own in states)

        zero = jnp.zeros((half_modes, lane_block), f32)
        states = lax.fori_loop(0, rows // step, body, (((zero, zero),) * 2,) * batches)
        for m in range(batches):
            for h in range(2):
                edge_ref[m, 0, h, :, lanes], edge_ref[m, 1, h, :, lanes] = states[m][h]

    each_block(share, on_lanes)


def load_states(ref, batches, lanes):
    return tuple(
        tuple((ref[m, 0, h, :, lanes], ref[m, 1, h, :, lanes]) for h in range(2)) for m in range(batches)
    )


def conv_kernel(batches, keep_ref, u_ref, into_ref, par_ref, skip_ref, y_ref, u_wide, y_wide):
    tokens, share = u_ref.shape
    rows = tokens // batches
    widen(u_ref, u_wide)

    def on_lanes(at, lanes):
        turn, res = (load_pairs(par_ref, 2 * i, lanes) for i in range(2))

        def body(block, states):
            states = [list(own) for own in states]
            for i in range(step):
                t = block * step + i
                for m in range(batches):
                    keep = keep_ref[m, t]
                    row = u_wide[at, pl.ds(m * rows + t, 1), :]
                    out = []
                    for h in range(2):
                        re, im = times(turn[h][0] * keep, turn[h][1] * keep, *states[m][h])
                        re = re + row
                        states[m][h] = (re, im)
                        out.append(res[h][0] * re - res[h][1] * im)
                    y_wide[at, pl.ds(m * rows + t, 1), :] = jnp.sum(out[0] + out[1], axis=0, keepdims=True)
            return tuple(tuple(own) for own in states)

        lax.fori_loop(0, rows // step, body, load_states(into_ref, batches, lanes))

    each_block(share, on_lanes)
    narrow(y_wide, u_wide, skip_ref, y_ref)


def back_kernel(
    batches,
    keep_ref,
    u_ref,
    g_ref,
    into_ref,
    behind_ref,
    par_ref,
    skip_ref,
    d_ref,
    sums_ref,
    skip_sum_ref,
    u_wide,
    g_wide,
    d_wide,
    kept,
):
    tokens, share = u_ref.shape
    rows = tokens // batches
    widen(u_ref, u_wide)
    widen(g_ref, g_wide)

    def on_lanes(at, lanes):
        turn, res = (load_pairs(par_ref, 2 * i, lanes) for i in range(2))

        def ahead(block, states):
            states = [list(own) for own in states]
            for i in range(step):
                t = block * step + i
                for m in range(batches):
                    keep = keep_ref[m, t]
                    row = u_wide[at, pl.ds(m * rows + t, 1), :]
                    for h in range(2):
                        re, im = times(turn[h][0] * keep, turn[h][1] * keep, *states[m][h])
                        kept[t, m, h, 0], kept[t, m, h, 1] = re, im
                        states[m][h] = (re + row, im)
            return tuple(tuple(own) for own in states)

        lax.fori_loop(0, rows // step, ahead, load_states(into_ref, batches, lanes))
        start = load_states(behind_ref, batches, lanes)

        def behind(block, carry):
            states, sums = [list(own) for own in carry[0]], list(carry[1])
            for i in range(step):
                t = rows - 1 - (block * step + i)
                for m in range(batches):
                    keep = keep_ref[m, t]
                    row = g_wide[at, pl.ds(m * rows + t, 1), :]
                    out = []
                    for h in range(2):
                        re, im = states[m][h]
                        re = re + row
                        x_re, x_im = kept[t, m, h, 0], kept[t, m, h, 1]
                        lag_re, lag_im = times(re, im, x_re, x_im)
                        g_re, g_im, w_re, w_im = sums[h]
                        sums[h] = (g_re + row * x_re, g_im + row * x_im, w_re + lag_re, w_im + lag_im)
                        out.append(res[h][0] * re - res[h][1] * im)
                        states[m][h] = times(turn[h][0] * keep, turn[h][1] * keep, re, im)
                    d_wide[at, pl.ds(m * rows + t, 1), :] = jnp.sum(out[0] + out[1], axis=0, keepdims=True)
            return tuple(tuple(own) for own in states), tuple(sums)

        zero = jnp.zeros((half_modes, lane_block), f32)
        skip_sum = jnp.sum(u_wide[at] * g_wide[at], axis=0, keepdims=True)
        skip_sum_ref[:, lanes] = skip_sum
        _, sums = lax.fori_loop(0, rows // step, behind, (start, ((zero,) * 4,) * 2))
        for h in range(2):
            g_re, g_im, w_re, w_im = sums[h]
            lag_re, lag_im = times(*res[h], w_re, w_im)
            sums_ref[0, h, :, lanes] = zero - lag_re
            sums_ref[1, h, :, lanes] = zero - lag_im
            sums_ref[2, h, :, lanes] = g_re + skip_sum
            sums_ref[3, h, :, lanes] = zero - g_im

    each_block(share, on_lanes)
    narrow(d_wide, g_wide, skip_ref, d_ref)


def in_vmem():
    return pl.BlockSpec(memory_space=pltpu.VMEM)


def in_smem():
    return pl.BlockSpec(memory_space=pltpu.SMEM)


def scratch_rows(u):
    return pltpu.VMEM((u.shape[1] // lane_block, u.shape[0], lane_block), f32)


def edge_states(u, keep, params, reverse):
    batches = keep.shape[0]
    return pl.pallas_call(
        functools.partial(edge_kernel, batches, reverse),
        out_shape=jax.ShapeDtypeStruct((batches, 2) + params.shape[1:], f32),
        in_specs=[in_smem(), in_vmem(), in_vmem()],
        out_specs=in_vmem(),
        scratch_shapes=[scratch_rows(u)],
        compiler_params=pltpu.CompilerParams(vmem_limit_bytes=48 << 20),
    )(keep, u, params)


def long_conv(keep, u, into, params, skips):
    return pl.pallas_call(
        functools.partial(conv_kernel, keep.shape[0]),
        out_shape=jax.ShapeDtypeStruct(u.shape, bf16),
        in_specs=[in_smem()] + [in_vmem()] * 4,
        out_specs=in_vmem(),
        scratch_shapes=[scratch_rows(u)] * 2,
        compiler_params=pltpu.CompilerParams(vmem_limit_bytes=48 << 20),
    )(keep, u, into, params, skips)


def long_conv_back(keep, u, g, into, behind, params, skips):
    batches, rows = keep.shape
    return pl.pallas_call(
        functools.partial(back_kernel, batches),
        out_shape=(
            jax.ShapeDtypeStruct(u.shape, bf16),
            jax.ShapeDtypeStruct((4,) + params.shape[1:], f32),
            jax.ShapeDtypeStruct((1, u.shape[1]), f32),
        ),
        in_specs=[in_smem()] + [in_vmem()] * 6,
        out_specs=(in_vmem(),) * 3,
        scratch_shapes=[scratch_rows(u)] * 3 + [pltpu.VMEM((rows, batches, 2, 2, half_modes, lane_block), f32)],
        compiler_params=pltpu.CompilerParams(vmem_limit_bytes=48 << 20),
    )(keep, u, g, into, behind, params, skips)


def shifted(array, axis, by):
    size = lax.axis_size(axis)
    pairs = [(i, i + by) for i in range(size) if 0 <= i + by < size]
    return lax.ppermute(array, axis, pairs)


def places_of(doc_lens, total):
    tokens = jnp.arange(total, dtype=jnp.int32)
    starts = jnp.cumsum(doc_lens, dtype=jnp.int32) - doc_lens
    begins = jnp.max(jnp.where(starts[None, :] <= tokens[:, None], starts[None, :], 0), axis=1)
    return tokens - begins


def dot_rows(left, right):
    return lax.dot_general(left, right, (((1,), (1,)), ((), ())), preferred_element_type=f32)


def dot_tokens(left, right):
    return lax.dot_general(left, right, (((0,), (0,)), ((), ())), preferred_element_type=f32)


def dot(left, right):
    return jnp.dot(left, right, preferred_element_type=f32)


def along_line(array, pairs):
    return lax.ppermute(array, "fsdp", pairs)


outer_pairs = [(0, 1), (1, 0), (2, 3), (3, 2)]
inner_pairs = [(1, 2), (2, 1)]


def after(value, *others):
    return lax.optimization_barrier((value,) + others)[0]


def gather_first(share):
    return along_line(share, outer_pairs), along_line(share, inner_pairs)


def gather_second(first):
    next_one, inner_one = first
    return along_line(inner_one, outer_pairs), along_line(next_one, inner_pairs)


def gather_last(second):
    return along_line(second[1], outer_pairs)


def gathered(share, first, second, last):
    own = lax.axis_index("fsdp")
    by_offset = (share, first[0], second[0] + second[1], last + first[1])
    blocks = []
    for place in range(4):
        offset = own ^ place
        block = by_offset[3]
        for k in range(3):
            block = jnp.where(offset == k, by_offset[k], block)
        blocks.append(block)
    return lax.optimization_barrier(jnp.concatenate(blocks, axis=1))


def gather_share(share):
    first = gather_first(share)
    second = gather_second(first)
    return gathered(share, first, second, gather_last(second))


def part_of(partial_sums, offset):
    share = partial_sums.shape[1] // 4
    return lax.dynamic_slice_in_dim(partial_sums, (lax.axis_index("fsdp") ^ offset) * share, share, 1)


def scatter_first(partial_sums):
    return along_line(part_of(partial_sums, 3), outer_pairs), along_line(part_of(partial_sums, 2), outer_pairs)


def scatter_second(partial_sums, first):
    far, near = first
    return (
        along_line(part_of(partial_sums, 2) + far, inner_pairs),
        along_line(part_of(partial_sums, 3) + near, inner_pairs),
    )


def scatter_last(partial_sums, second):
    return along_line(part_of(partial_sums, 1) + second[0], outer_pairs)


def scattered(partial_sums, second, last):
    return part_of(partial_sums, 0).astype(f32) + last.astype(f32) + second[1].astype(f32)


def scatter_offloaded(partial_sums):
    return lax.psum_scatter(partial_sums, "fsdp", scatter_dimension=1, tiled=True).astype(f32)


def sum_line(array):
    array = array + along_line(array, outer_pairs)
    return array + along_line(array, [(i, i ^ 2) for i in range(4)])


def swap_seq(array, bit):
    return lax.ppermute(array, "seq", [(i, i ^ (1 << bit)) for i in range(lax.axis_size("seq"))])


def gather_weight(shard):
    return lax.all_gather(shard, "seq", axis=0, tiled=True)


def of_core(left, core):
    count = lax.axis_size("seq")
    rows = left.shape[1] // count
    parts = [lax.dynamic_slice_in_dim(left, (2 * chip + core) * rows, rows, 1) for chip in range(count // 2)]
    return lax.optimization_barrier(jnp.concatenate(parts, axis=1))


def core_give(left, right):
    core = lax.axis_index("seq") % 2
    return lax.optimization_barrier(dot_tokens(of_core(left, 1 - core), right).astype(bf16))


def core_sum(left, right, got):
    own = dot_tokens(of_core(left, lax.axis_index("seq") % 2), right)
    return with_layout_constraint((own + got.astype(f32)).astype(bf16), Layout(major_to_minor=(0, 1)))


def chip_sums_offloaded(summed):
    count = lax.axis_size("seq")
    groups = [list(range(core, count, 2)) for core in range(2)]
    return lax.psum_scatter(summed, "seq", scatter_dimension=0, axis_index_groups=groups, tiled=True)


def chip_sums(summed, *before_last):
    count = lax.axis_size("seq")
    rank = lax.axis_index("seq")
    rows, bits = 2 * summed.shape[0] // count, count.bit_length() - 1
    by_bits = summed.reshape((2,) * (bits - 1) + (rows, summed.shape[1]))

    def halve(array, rest, bit):
        dim, mine = rest.index(bit), (rank >> bit) & 1
        keep = lax.dynamic_index_in_dim(array, mine, dim, keepdims=False)
        give = lax.dynamic_index_in_dim(array, 1 - mine, dim, keepdims=False)
        got = swap_seq(give.astype(bf16), bit)
        return keep.astype(f32) + got.astype(f32), [other for other in rest if other != bit]

    chip_bits = list(range(1, bits))
    middle = len(chip_bits) // 2
    parts = []
    for half, order in enumerate((chip_bits, chip_bits[middle:] + chip_bits[:middle])):
        part = lax.slice_in_dim(by_bits, half * rows // 2, (half + 1) * rows // 2, axis=bits - 1)
        rest = chip_bits[::-1]
        for bit in order[:-1]:
            part, rest = halve(part, rest, bit)
        part, rest = halve(after(part.astype(bf16), *before_last) if before_last else part, rest, order[-1])
        parts.append(with_layout_constraint(part, Layout(major_to_minor=(0, 1))))
    return parts


def passing_factors(whole, power, reverse):
    count = lax.axis_size("seq")
    rank = lax.axis_index("seq")
    if reverse:
        rank, whole = count - 1 - rank, whole[:, ::-1]
    devices = jnp.arange(count)

    def factor(exponent, within):
        kept = jnp.min(jnp.where(within, whole, 1.0), axis=1)[:, None, None, None]
        return jnp.stack([part * kept for part in power(exponent)])

    steps = []
    for bit in range(count.bit_length() - 1):
        size = 1 << bit
        group = rank // size
        later = (group % 2).astype(f32)
        ahead = factor((rank % size).astype(f32), (devices // size == group) & (devices < rank)) * later
        last = factor(float(size), devices // size == (group | 1))
        steps.append((ahead, last))
    return lax.optimization_barrier(steps)


def through(edge, factors, reverse):
    count = lax.axis_size("seq")
    rank = lax.axis_index("seq")
    if reverse:
        rank = count - 1 - rank

    def grown(factor, state):
        re, im = times(factor[0], factor[1], state[:, 0], state[:, 1])
        return jnp.stack([re, im], axis=1)

    into = jnp.zeros_like(edge)
    for bit, (ahead, last) in enumerate(factors):
        later = (rank >> bit) & 1 == 1
        got = swap_seq(edge, bit)
        into = into + grown(ahead, got)
        if bit + 1 < len(factors):
            edge = jnp.where(later, edge, got) + grown(last, jnp.where(later, got, edge))
    return into


def sum_seq(array):
    for bit in range(lax.axis_size("seq").bit_length() - 1):
        array = array + swap_seq(array, bit)
    return array


def on_device(
    hidden_in,
    out_cot,
    doc_lengths,
    mixer_gain,
    in_proj,
    short_filter,
    decay_rate,
    mode_angle,
    residue_re,
    residue_im,
    skip_gain,
    out_proj,
    feed_gain,
    gate_proj,
    up_proj,
    down_proj,
):
    batches, rows, share = hidden_in.shape
    tokens = batches * rows
    width = mixer_gain.shape[0]
    seq_count = lax.axis_size("seq")
    seq_rank = lax.axis_index("seq")
    fsdp_rank = lax.axis_index("fsdp")
    total = rows * seq_count
    d_rows = in_proj.shape[0]

    x_share = hidden_in.reshape(tokens, share)
    cot_share = out_cot.reshape(tokens, share)
    x_rows = gather_share(x_share)
    x_all = x_rows.astype(f32)
    units = gate_proj.shape[1]
    w_in = gather_weight(jnp.concatenate([in_proj[:, j] for j in range(3)], axis=1))
    w_both = gather_weight(jnp.concatenate([out_proj.T, down_proj.T], axis=1))
    w_out, w_down = w_both[:, :share], w_both[:, share:]
    w_feed = gather_weight(jnp.concatenate([gate_proj, up_proj], axis=1))

    places = jnp.stack([places_of(doc_lengths[m], total) for m in range(batches)])
    keep = (places > 0).astype(f32)
    places_here = lax.dynamic_slice_in_dim(places, seq_rank * rows, rows, 1)
    masks = [(places_here >= lag).astype(f32)[:, :, None] for lag in range(3)]
    taps = short_filter.reshape(3, 3 * share)

    keep_here = lax.dynamic_slice_in_dim(keep, seq_rank * rows, rows, 1)
    whole = jnp.min(keep.reshape(batches, seq_count, rows), axis=2)
    rates, angles, res_re, res_im = (
        part.T.reshape(2, half_modes, share) for part in (decay_rate, mode_angle, residue_re, residue_im)
    )

    def power(devices):
        fading = jnp.exp(-(devices * rows) * rates)
        return fading * jnp.cos((devices * rows) * angles), fading * jnp.sin((devices * rows) * angles)

    fading = jnp.exp(-rates)
    modes = jnp.stack([fading * jnp.cos(angles), fading * jnp.sin(angles), res_re, res_im])
    skips = skip_gain[None]
    masked_taps = lax.optimization_barrier([taps[lag] * masks[lag] for lag in range(3)])
    factors = passing_factors(whole, power, False)
    back_factors = passing_factors(whole, power, True)

    scale_one = lax.rsqrt(jnp.mean(x_all * x_all, axis=-1, keepdims=True) + norm_eps)
    unit_one = x_all * scale_one
    normed_one = after((unit_one * mixer_gain).astype(bf16), modes, masked_taps, factors, back_factors)
    project = dot(normed_one, w_in).reshape(batches, rows, 3 * share)
    extended = jnp.concatenate([shifted(project[:, -2:], "seq", 1), project], axis=1)
    lagged = [extended[:, 2 - lag : 2 - lag + rows] for lag in range(3)]
    conv = sum(masked_taps[lag] * lagged[lag] for lag in range(3)).reshape(tokens, 3 * share)
    gate_one, gate_two, values = (conv[:, j * share : (j + 1) * share] for j in range(3))
    product = (gate_two * values).astype(bf16)
    cot_late = after(cot_share, product)
    cot_first = gather_first(cot_late)
    into = through(edge_states(product, keep_here, modes, False), factors, False)
    cot_second = gather_second(cot_first)
    mixed = long_conv(keep_here, product, after(into, *cot_first), modes, skips)
    cot_last = gather_last(cot_second)
    mixed = after(mixed, *cot_second).astype(f32)
    gated = (gate_one * mixed).astype(bf16)
    mix_part = dot_rows(gated, w_out).astype(bf16)
    mix_first = scatter_first(mix_part)
    mix_second = scatter_second(mix_part, mix_first)
    cot_all = gathered(cot_share, cot_first, cot_second, after(cot_last, mix_first[0]))
    d_hidden = lax.optimization_barrier(dot(cot_all, w_down))
    mix_last = scatter_last(mix_part, mix_second)
    stream = x_share.astype(f32) + scattered(mix_part, mix_second, mix_last)
    stream_all = gather_share(stream.astype(bf16)).astype(f32)
    scale_two = lax.rsqrt(jnp.mean(stream_all * stream_all, axis=-1, keepdims=True) + norm_eps)
    unit_two = stream_all * scale_two
    normed_two = lax.optimization_barrier((unit_two * feed_gain).astype(bf16))
    feed_pre = dot(normed_two, w_feed)
    gate_pre, up_pre = feed_pre[:, :units], feed_pre[:, units:]
    sigmoid = jax.nn.sigmoid(gate_pre)
    activated = gate_pre * sigmoid
    hidden = (activated * up_pre).astype(bf16)

    d_gate = d_hidden * up_pre * sigmoid * (1.0 + gate_pre * (1.0 - sigmoid))
    d_up = d_hidden * activated
    d_gate_low, d_up_low = d_gate.astype(bf16), d_up.astype(bf16)
    along_two = jnp.sum(d_gate * gate_pre + d_up * up_pre, axis=-1)
    along_two = sum_line(along_two.reshape(-1, 128))
    part_two = (dot_rows(d_gate_low, w_feed[:, :units]) + dot_rows(d_up_low, w_feed[:, units:])).astype(bf16)
    d_feed = jnp.concatenate(lax.optimization_barrier((d_gate_low, d_up_low, part_two))[:2], axis=1)
    along_two = along_two.reshape(tokens, 1)
    dn_two = lax.psum_scatter(part_two, "fsdp", scatter_dimension=1, tiled=True)
    feed_got = swap_seq(core_give(normed_two, after(d_feed, part_two)), 0)
    down_got = swap_seq(core_give(cot_all, after(hidden, part_two)), 0)
    feed_sum = core_sum(normed_two, d_feed, feed_got)
    down_sum = core_sum(cot_all, hidden, down_got)

    def own_features(part):
        return lax.dynamic_slice_in_dim(part, fsdp_rank * share, share, 0)

    d_stream = (
        cot_share.astype(f32)
        + scale_two * own_features(feed_gain) * dn_two.astype(f32)
        - stream * (scale_two * scale_two * along_two / width)
    )
    d_share = d_stream.astype(bf16)
    d_mix = lax.all_gather(d_share, "fsdp", axis=1, tiled=True)
    down_part = dot_rows(after(hidden, d_share), w_down).astype(bf16)
    feed_sums = lax.optimization_barrier(jnp.concatenate([feed_sum, down_sum], axis=1))
    d_mix = after(d_mix, feed_sums, down_part)
    feed_own = chip_sums_offloaded(after(feed_sums, d_mix))

    d_gated = lax.optimization_barrier(dot(d_mix, w_out))
    down_first = scatter_first(after(down_part, d_gated))
    d_gate_one = d_gated * mixed
    d_mixed = (d_gated * gate_one).astype(bf16)
    behind = through(edge_states(d_mixed, keep_here, modes, True), back_factors, True)
    down_second = scatter_second(down_part, down_first)
    d_mix_late = after(d_mix, d_mixed)
    out_sum = core_sum(d_mix_late, gated, swap_seq(core_give(d_mix_late, gated), 0))
    down_last = scatter_last(down_part, down_second)
    feed_gain_part = jnp.sum(unit_two * after(part_two, d_mixed).astype(f32), axis=0)
    d_product, mode_sums, skip_sums = long_conv_back(
        keep_here, product, d_mixed, into, after(behind, *down_first), modes, skips
    )
    d_product = after(d_product, out_sum, feed_gain_part, *down_second)
    block_out = stream + scattered(down_part, down_second, down_last)
    d_product = d_product.astype(f32)
    d_conv = jnp.concatenate([d_gate_one, d_product * values, d_product * gate_two], axis=1)
    d_conv = d_conv.reshape(batches, rows, 3 * share)
    spread = sum(
        jnp.pad(taps[lag] * masks[lag] * d_conv, ((0, 0), (2 - lag, lag), (0, 0))) for lag in range(3)
    )
    returned = shifted(spread[:, :2], "seq", -1)
    d_project = spread[:, 2:] + jnp.pad(returned, ((0, 0), (rows - 2, 0), (0, 0)))
    d_project = d_project.astype(bf16).reshape(tokens, 3 * share)
    part_one = dot_rows(d_project, w_in).astype(bf16)
    dn_one = lax.psum_scatter(after(part_one, feed_own), "fsdp", scatter_dimension=1, tiled=True)
    in_give = core_give(normed_one, after(d_project, part_one))
    in_got = swap_seq(in_give, 0)
    in_sum = core_sum(normed_one, d_project, in_got)
    in_out = chip_sums(jnp.concatenate([in_sum, out_sum], axis=1), dn_one)
    d_conv, late_project, late_part = lax.optimization_barrier((d_conv, d_project, part_one, in_sum, feed_own))[:3]
    short_part = jnp.stack([jnp.sum(masks[lag] * lagged[lag] * d_conv, axis=(0, 1)) for lag in range(3)])
    mixer_gain_part = jnp.sum(unit_one * late_part.astype(f32), axis=0)
    small = [mixer_gain_part, feed_gain_part, short_part, mode_sums, skip_sums]
    small = jnp.concatenate([part.reshape(-1, share) for part in small])
    for bit in range(1, seq_count.bit_length() - 1):
        small = small + swap_seq(small, bit)
    feed_own = after(feed_own, in_sum)
    gate_grad, up_grad, down_grad = (
        feed_own[:, i * units : (i + 1) * units].astype(f32) for i in range(3)
    )
    small = small
    small = small + swap_seq(small, 0)
    gain_rows = 2 * width // share
    along_one = jnp.sum(late_project.astype(f32) * project.reshape(tokens, 3 * share), axis=-1)
    lined = sum_line(jnp.concatenate([small[:gain_rows], along_one.reshape(-1, share)]))
    gains, along_one = lined[:gain_rows].reshape(2, width), lined[gain_rows:].reshape(tokens, 1)
    d_x = (
        d_stream
        + scale_one * own_features(mixer_gain) * dn_one.astype(f32)
        - x_share.astype(f32) * (scale_one * scale_one * along_one / width)
    )

    branches = [jnp.concatenate([half[:, j * share : (j + 1) * share] for half in in_out]) for j in range(4)]
    in_grad, out_grad = jnp.stack(branches[:3]).transpose(1, 0, 2), branches[3]
    short_grad = small[gain_rows : gain_rows + 9].reshape(3, 3, share)
    filters = small[gain_rows + 9 :]
    by_chan = filters[:-1].reshape(4, 2 * half_modes, share).transpose(0, 2, 1)
    return (
        block_out.astype(bf16).reshape(hidden_in.shape),
        d_x.reshape(hidden_in.shape),
        gains[0],
        in_grad,
        short_grad,
        by_chan[0],
        by_chan[1],
        by_chan[2],
        by_chan[3],
        filters[-1],
        out_grad.T,
        gains[1],
        gate_grad,
        up_grad,
        down_grad.T,
    )


def solution(mesh):
    tokens = P(None, "seq", "fsdp")
    chan_rows = P("fsdp", None)
    d_rows = P("seq", "fsdp")
    d_cols = P("fsdp", "seq")
    in_specs = (
        tokens,
        tokens,
        P(),
        P(),
        P("seq", None, "fsdp"),
        P(None, None, "fsdp"),
        chan_rows,
        chan_rows,
        chan_rows,
        chan_rows,
        P("fsdp"),
        d_cols,
        P(),
        d_rows,
        d_rows,
        d_cols,
    )
    out_specs = (
        tokens,
        tokens,
        P(),
        P("seq", None, "fsdp"),
        P(None, None, "fsdp"),
        chan_rows,
        chan_rows,
        chan_rows,
        chan_rows,
        P("fsdp"),
        d_cols,
        P(),
        d_rows,
        d_rows,
        d_cols,
    )
    return jax.shard_map(on_device, mesh=mesh, in_specs=in_specs, out_specs=out_specs, check_vma=False)
```
